512 devices in a mesh: ply: 2 (over x_lo), len: 16 (over y, core), hgt: 16 (over x_hi, z).
Axes of the slice: x: 4 (x_hi: 2, x_lo: 2; x = x_hi * 2 + x_lo), y: 8, z: 8, core: 2. Of those that a mesh axis runs over, the one named last changes fastest.
Arguments:
- plate_state: float32 [2, 10, 8, 256, 2048], P('ply', None, None, 'len', 'hgt'), may hold values from -6 to 6
- damage: int32 [2, 8, 256, 2048], P('ply', None, 'len', 'hgt'), may hold values from 0 to 4
- frame_mask: int32 [256, 2048], P('len', 'hgt'), may hold values 0 or 1
- impact_mask: int32 [256, 2048], P('len', 'hgt'), may hold values 0 or 1
Outputs:
- final_state: float32 [2, 10, 8, 256, 2048], P('ply', None, None, 'len', 'hgt')
The draws below stay inside these ranges and needn't reach their ends.
All inputs are finite; a program needn't handle non-finite values. No bound on the sum of `frame_mask` or of `impact_mask` on one device may be relied on, other than what follows from the above.
Results may differ from the reference program's by a relative error of at most 0.0001.
Values sent between devices are 32-bit elements; how exact they have to be, the bound alone decides.
No kernel may reach another device: no remote copies, remote signals or barrier semaphores. Data moves between devices by JAX's collectives and lax.ppermute only.
A program may use at most 64 MiB of HBM per device.

```python
import jax
import jax.numpy as jnp
from jax import lax

FIELDS = 10
NZ = 8
STEPS = 2
NL = 256
NH = 2048


def with_ends(entries, stream_key, smallest, top_value):
    index_at = [jax.random.randint(jax.random.fold_in(stream_key, axis), (), 0, length) for axis, length in enumerate(entries.shape)]
    widest = entries.shape.index(max(entries.shape))
    neighbour = index_at[:widest] + [(index_at[widest] + 1) % entries.shape[widest]] + index_at[widest + 1:]
    return entries.at[tuple(index_at)].set(smallest).at[tuple(neighbour)].set(top_value)


def shard_levels(own_key, dims, shards, least, high):
    factor_of = 1.0
    for position, blocks in shards:
        heights = jax.random.uniform(jax.random.fold_in(jax.random.fold_in(own_key, 6), position), (blocks,), jnp.float32, least / len(shards), high / len(shards))
        factor_of = factor_of * jnp.repeat(jnp.exp(heights), dims[position] // blocks).reshape((-1,) + (1,) * (len(dims) - 1 - position))
    return factor_of


def scatter_about(rng, extent, width, bound, pieces=(), held_as=jnp.bfloat16):
    factor_of = shard_levels(rng, extent, pieces, -0.22, 0.18) if pieces else 1.0
    entries = jax.random.normal(rng, extent, jnp.float32) * width * factor_of
    return jnp.minimum(jnp.maximum(entries, -bound), bound).astype(held_as)


def setup_inputs(seed: int = 0) -> dict:
    keys = jax.random.split(jax.random.key(seed), 5)
    plate_state = scatter_about(keys[0], (2, FIELDS, NZ, NL, NH), 1.0, 6.0, ((0, 2), (3, 16), (4, 16)), jnp.float32)
    damage = with_ends(jax.random.randint(keys[1], (2, NZ, NL, NH), 0, 5), jax.random.fold_in(keys[1], 1), 0, 4).astype(jnp.int32)
    frame_mask = with_ends((jax.random.randint(keys[2], (NL, NH), 0, 8) < 1).astype(jnp.int32), jax.random.fold_in(keys[2], 1), 0, 1)
    impact_mask = with_ends((jax.random.randint(keys[3], (NL, NH), 0, 4) < 1).astype(jnp.int32), jax.random.fold_in(keys[3], 1), 0, 1)
    return {"plate_state": plate_state, "damage": damage, "frame_mask": frame_mask, "impact_mask": impact_mask}


time_step = 0.25
softening = 0.15
damping = 1.0
stiffness = 2.0
pressure = 2.0


def central(field, axis, count):
    def shifted(offset):
        return lax.slice_in_dim(field, 2 + offset, 2 + offset + count, axis=axis)
    return (8.0 * (shifted(1) - shifted(-1)) - (shifted(2) - shifted(-2))) / 12.0


def along_length(field):
    return central(field, 1, field.shape[1] - 4)[:, :, 2:-2]


def along_height(field):
    return central(field, 2, field.shape[2] - 4)[:, 2:-2, :]


def through_thickness(field):
    padded = jnp.pad(field[:, 2:-2, 2:-2], ((2, 2), (0, 0), (0, 0)))
    return central(padded, 0, field.shape[0])


def layer_weights(thick, ply_index):
    layer = jnp.arange(thick)
    bonded = jnp.where(layer == jnp.where(ply_index == 0, thick - 1, 0), 1.0, 0.0).astype(jnp.float32)
    outer = jnp.where((layer == 0) & (ply_index == 0), 1.0, 0.0).astype(jnp.float32)
    return bonded, outer


def surface_of(velocity, normal_disp, ply_index):
    bonded, outer = layer_weights(velocity.shape[1], ply_index)
    selected = jnp.concatenate([velocity, normal_disp[None]], axis=0)
    return jnp.sum(selected * bonded[None, :, None, None], axis=1)


def velocity_update(stress_pad, velocity, normal_disp, partner, keep_mask, push_mask, ply_index):
    bonded, outer = layer_weights(velocity.shape[1], ply_index)
    own = surface_of(velocity, normal_disp, ply_index)
    accel_x = along_length(stress_pad[0]) + along_height(stress_pad[3]) + through_thickness(stress_pad[4])
    accel_y = along_length(stress_pad[3]) + along_height(stress_pad[1]) + through_thickness(stress_pad[5])
    accel_z = along_length(stress_pad[4]) + along_height(stress_pad[5]) + through_thickness(stress_pad[2])
    accel_z = accel_z + pressure * push_mask[None] * outer[:, None, None]
    pull_x = damping * (partner[0] - own[0])
    pull_y = damping * (partner[1] - own[1])
    pull_z = stiffness * (partner[3] - own[3]) + damping * (partner[2] - own[2])
    traction = jnp.stack([pull_x, pull_y, pull_z])[:, None] * bonded[None, :, None, None]
    accel = jnp.stack([accel_x, accel_y, accel_z]) + traction
    return (velocity + time_step * accel) * keep_mask[None, None]


def stress_update(stress, vel_pad, levels):
    scale = 1.0 - softening * levels.astype(jnp.float32)
    lame_local = scale
    shear_local = scale
    grad_xx = along_length(vel_pad[0])
    grad_yy = along_height(vel_pad[1])
    grad_zz = through_thickness(vel_pad[2])
    divergence = grad_xx + grad_yy + grad_zz
    shear_xy = along_height(vel_pad[0]) + along_length(vel_pad[1])
    shear_xz = through_thickness(vel_pad[0]) + along_length(vel_pad[2])
    shear_yz = through_thickness(vel_pad[1]) + along_height(vel_pad[2])
    change = jnp.stack([
        lame_local * divergence + 2.0 * shear_local * grad_xx,
        lame_local * divergence + 2.0 * shear_local * grad_yy,
        lame_local * divergence + 2.0 * shear_local * grad_zz,
        shear_local * shear_xy,
        shear_local * shear_xz,
        shear_local * shear_yz])
    return stress + time_step * change


def finish(fields, vel_pad, levels):
    stress_new = stress_update(fields[3:9], vel_pad, levels)
    velocity = vel_pad[:, :, 2:-2, 2:-2]
    normal_disp = fields[9] + time_step * velocity[2]
    return jnp.concatenate([velocity, stress_new, normal_disp[None]], axis=0)


def pad_plane(field):
    return jnp.pad(field, ((0, 0), (0, 0), (2, 2), (2, 2)))


def reference(plate_state, damage, frame_mask, impact_mask):
    keep_mask = (1 - frame_mask).astype(jnp.float32)
    push_mask = impact_mask.astype(jnp.float32)
    fields = [plate_state[0], plate_state[1]]
    for step_index in range(STEPS):
        surfaces = [surface_of(fields[0][0:3], fields[0][9], 0), surface_of(fields[1][0:3], fields[1][9], 1)]
        updated = []
        for ply_index in range(2):
            current = fields[ply_index]
            velocity = velocity_update(pad_plane(current[3:9]), current[0:3], current[9], surfaces[1 - ply_index], keep_mask, push_mask, ply_index)
            updated.append(finish(current, pad_plane(velocity), damage[ply_index]))
        fields = updated
    return jnp.stack(fields)
```

```python
import functools

import jax
import jax.numpy as jnp
from jax import lax
from jax.experimental import pallas as pl
from jax.experimental.pallas import tpu as pltpu
from jax.sharding import PartitionSpec as P

time_step = 0.25
softening = 0.15
damping = 1.0
stiffness = 2.0
pressure = 2.0

THICK = 8
ROWS = 16
LANES = 128
HALO = 8
EXT = ROWS + 2 * HALO

SCALE = 72
DISP = 80
MATE = 81
KEEP = 96
PUSH = 97
PLANES = 98
PER_GROUP = 16
GROUPS = 7

STORE = 48
TOP = 16

STRIDE = THICK + 2
VX, VY, VZ, SXX, SYY, SZZ, SXY, SXZ, SYZ = range(9)
FIELD_PLANES = 9 * STRIDE + 2

VMEM = pl.BlockSpec(memory_space=pltpu.VMEM)
PAIRS_EVEN = [[2 * i, 2 * i + 1] for i in range(8)]


def pair_groups(count, first):
    return [[(i + first) % count, (i + first + 1) % count] for i in range(0, count, 2)]


def surface_kernel(state, out):
    front = lax.axis_index("ply") == 0

    def layer(field, depth):
        return jnp.where(front, state[0, field, THICK - 1 - depth], state[0, field, depth])

    picks = [(f, 0) for f in (0, 1, 2, 9, 3, 4, 6, 7, 8)]
    picks += [(f, depth) for depth in (1, 2) for f in (7, 8, 5)]
    for k, (field, depth) in enumerate(picks):
        out[k] = layer(field, depth)


def write_tile(state, damage, frame, impact, mate, out, rows, size, front):
    for field in range(9):
        for z in range(THICK):
            out(field * THICK + z, state[0, field, z, rows, :])
    for z in range(THICK):
        out(SCALE + z, 1.0 - softening * damage[0, z, rows, :].astype(jnp.float32))
    out(DISP, jnp.where(front, state[0, 9, THICK - 1, rows, :], state[0, 9, 0, rows, :]))
    for k in range(15):
        out(MATE + k, jnp.where(front, mate[1, k, rows, :], mate[0, k, rows, :]))
    out(KEEP, (1 - frame[rows, :]).astype(jnp.float32))
    out(PUSH, impact[rows, :].astype(jnp.float32))


def length_kernel(state, damage, frame, impact, mate, near, far):
    front = lax.axis_index("ply") == 0
    core = lax.axis_index("len") % 2
    for out, start in ((near, (1 - core) * HALO), (far, core * HALO)):
        rows = pl.ds(pl.multiple_of(start, HALO), HALO)

        def put(plane, value, out=out):
            out[plane] = value

        write_tile(state, damage, frame, impact, mate, put, rows, HALO, front)


def height_kernel(state, damage, frame, impact, mate, near, far, ext, right, left):
    front = lax.axis_index("ply") == 0
    index = lax.axis_index("len")
    core = index % 2
    has_top = index > 0
    has_bottom = index < lax.axis_size("len") - 1

    def put(plane, value):
        ext[plane, HALO : HALO + ROWS, :] = value

    write_tile(state, damage, frame, impact, mate, put, slice(0, ROWS), ROWS, front)
    for plane in range(PLANES):
        top = jnp.where(core == 0, far[0, plane], near[0, plane])
        bottom = jnp.where(core == 0, near[1, plane], far[1, plane])
        ext[plane, 0:HALO, :] = jnp.where(has_top, top, 0.0)
        ext[plane, HALO + ROWS : EXT, :] = jnp.where(has_bottom, bottom, 0.0)
    slot = lax.broadcasted_iota(jnp.int32, (EXT, LANES), 1) // HALO
    for g in range(GROUPS):
        first = jnp.zeros((EXT, LANES), jnp.float32)
        last = first
        for j in range(min(PER_GROUP, PLANES - g * PER_GROUP)):
            plane = ext[g * PER_GROUP + j]
            head = pltpu.roll(plane, HALO * j, 1) if j else plane
            tail = pltpu.roll(plane, (HALO * j + HALO) % LANES, 1) if j < 15 else plane
            first = jnp.where(slot == j, head, first)
            last = jnp.where(slot == j, tail, last)
        left[g] = first
        right[g] = last


def lane_shift(x, s):
    lane = lax.broadcasted_iota(jnp.int32, x.shape, 2)
    turned = pltpu.roll(x, (-s) % LANES, 2)
    other = jnp.concatenate([turned[1:2], turned[0:1]], axis=0)
    inside = lane < LANES - s if s > 0 else lane >= -s
    return jnp.where(inside, turned, other)


def along_height(x):
    a = x - lane_shift(x, -2)
    b = 8.0 * a - lane_shift(a, 1)
    return lane_shift(b, 1) - a


def main_kernel(state, ext, near, far, out, fields, scale, extra):
    front = lax.axis_index("ply") == 0
    place = lax.axis_index("hgt")
    odd = place % 2
    has_left = place > 0
    has_right = place < lax.axis_size("hgt") - 1
    bonded = jnp.where(front, THICK - 1, 0)
    rows_all = slice(TOP - HALO, TOP + ROWS + HALO)

    zero = jnp.zeros((2, STORE, LANES), jnp.float32)
    for f in range(10):
        fields[f * STRIDE] = zero
        fields[f * STRIDE + 1] = zero

    lane = lax.broadcasted_iota(jnp.int32, (EXT, LANES), 1)
    is_right = (lane < HALO) & has_right
    is_left = (lane >= LANES - HALO) & has_left
    for g in range(GROUPS):
        from_right = jnp.where(odd == 0, near[1, g], far[1, g])
        from_left = jnp.where(odd == 0, far[0, g], near[0, g])
        for j in range(min(PER_GROUP, PLANES - g * PER_GROUP)):
            plane = g * PER_GROUP + j
            r = pltpu.roll(from_right, LANES - HALO * j, 1) if j else from_right
            m = pltpu.roll(from_left, LANES - HALO - HALO * j, 1) if j < 15 else from_left
            side = jnp.where(is_right, r, jnp.where(is_left, m, 0.0))
            if plane < SCALE:
                ref, at = fields, plane // THICK * STRIDE + 2 + plane % THICK
            elif plane < DISP:
                ref, at = scale, plane - SCALE
            else:
                ref, at = extra, plane - DISP
            ref[at, 0, rows_all, :] = ext[plane]
            ref[at, 1, rows_all, :] = side

    mate_at, keep_at, push_at = MATE - DISP, KEEP - DISP, PUSH - DISP
    step = time_step / 12.0

    def along_length(ref, at, r0, n):
        def tap(d):
            return ref[at, :, r0 + d : r0 + d + n, :]

        return 8.0 * (tap(1) - tap(-1)) - (tap(2) - tap(-2))

    def through(f, z, r0, n):
        def tap(d):
            return fields[f * STRIDE + 2 + z + d, :, r0 : r0 + n, :]

        return 8.0 * (tap(1) - tap(-1)) - (tap(2) - tap(-2))

    def spot(f, z):
        return f * STRIDE + 2 + z

    def velocities(r0, n, with_mate):
        keep = extra[keep_at, :, r0 : r0 + n, :]
        own = [fields[spot(f, bonded), :, r0 : r0 + n, :] for f in (VX, VY, VZ)]
        own.append(extra[0, :, r0 : r0 + n, :])
        mate = [extra[mate_at + k, :, r0 : r0 + n, :] for k in range(4)]
        pull = [
            damping * (mate[0] - own[0]),
            damping * (mate[1] - own[1]),
            stiffness * (mate[3] - own[3]) + damping * (mate[2] - own[2]),
        ]

        def body(z, carry):
            for v, a, b, c in ((VX, SXX, SXY, SXZ), (VY, SXY, SYY, SYZ), (VZ, SXZ, SYZ, SZZ)):
                total = (
                    along_length(fields, spot(a, z), r0, n)
                    + along_height(fields[spot(b, z), :, r0 : r0 + n, :])
                    + through(c, z, r0, n)
                )
                old = fields[spot(v, z), :, r0 : r0 + n, :]
                fields[spot(v, z), :, r0 : r0 + n, :] = (old + step * total) * keep
            return carry

        lax.fori_loop(0, THICK, body, 0)
        for f in range(3):
            at = spot(f, bonded)
            fields[at, :, r0 : r0 + n, :] += time_step * pull[f] * keep
        push = extra[push_at, :, r0 : r0 + n, :] * keep
        at = spot(VZ, 0)
        fields[at, :, r0 : r0 + n, :] += jnp.where(front, time_step * pressure, 0.0) * push

        if with_mate:
            sign = jnp.where(front, 1.0, -1.0)
            inner = lambda k: extra[mate_at + k, :, r0 : r0 + n, :]
            fresh = []
            for f, (a, b, one, two) in enumerate(((4, 6, 9, 12), (6, 5, 10, 13), (7, 8, 11, 14))):
                total = (
                    along_length(extra, mate_at + a, r0, n)
                    + along_height(extra[mate_at + b, :, r0 : r0 + n, :])
                    + sign * (8.0 * inner(one) - inner(two))
                )
                fresh.append((mate[f] + step * total - time_step * pull[f]) * keep)
            for f in range(3):
                extra[mate_at + f, :, r0 : r0 + n, :] = fresh[f]
            extra[mate_at + 3, :, r0 : r0 + n, :] = mate[3] + time_step * fresh[2]
            extra[0, :, r0 : r0 + n, :] = (
                own[3] + time_step * fields[spot(VZ, bonded), :, r0 : r0 + n, :]
            )

    def changes(z, r0, n, size):
        def cut(x):
            return x[:size]

        def length_of(f):
            return cut(along_length(fields, spot(f, z), r0, n))

        def height_of(f):
            return cut(along_height(fields[spot(f, z), :, r0 : r0 + n, :]))

        def depth_of(f):
            return cut(through(f, z, r0, n))

        factor = step * scale[z, 0:size, r0 : r0 + n, :]
        xx, yy, zz = length_of(VX), height_of(VY), depth_of(VZ)
        whole = xx + yy + zz
        return (
            factor * (whole + 2.0 * xx),
            factor * (whole + 2.0 * yy),
            factor * (whole + 2.0 * zz),
            factor * (height_of(VX) + length_of(VY)),
            factor * (depth_of(VX) + length_of(VZ)),
            factor * (depth_of(VY) + height_of(VZ)),
        )

    velocities(TOP - HALO, EXT, True)

    def first_stress(z, carry):
        r0, n = TOP - 4, ROWS + 8
        for f, change in enumerate(changes(z, r0, n, 2)):
            fields[spot(SXX + f, z), :, r0 : r0 + n, :] += change
        out[0, 9, z] = state[0, 9, z] + time_step * fields[spot(VZ, z), 0, TOP : TOP + ROWS, :]
        return carry

    lax.fori_loop(0, THICK, first_stress, 0)
    velocities(TOP - 4, ROWS + 8, False)

    def last_stress(z, carry):
        for f in range(3):
            out[0, f, z] = fields[spot(f, z), 0, TOP : TOP + ROWS, :]
        for f, change in enumerate(changes(z, TOP, ROWS, 1)):
            out[0, 3 + f, z] = fields[spot(SXX + f, z), 0, TOP : TOP + ROWS, :] + change[0]
        out[0, 9, z] += time_step * fields[spot(VZ, z), 0, TOP : TOP + ROWS, :]
        return carry

    lax.fori_loop(0, THICK, last_stress, 0)


def shaped(*shape):
    return jax.ShapeDtypeStruct(shape, jnp.float32)


def call(kernel, outs, args, **more):
    return pl.pallas_call(
        kernel,
        out_shape=outs,
        in_specs=[VMEM] * len(args),
        out_specs=jax.tree.map(lambda _: VMEM, outs),
        compiler_params=pltpu.CompilerParams(vmem_limit_bytes=32 * 2**20),
        **more,
    )(*args)


def per_device(plate_state, damage, frame_mask, impact_mask):
    even, odd = pair_groups(16, 0), pair_groups(16, 1)
    surface = call(surface_kernel, shaped(15, ROWS, LANES), (plate_state,))
    mate = lax.all_gather(surface, "ply")
    local = (plate_state, damage, frame_mask, impact_mask, mate)
    near, far = call(length_kernel, [shaped(PLANES, HALO, LANES)] * 2, local)
    near = lax.all_gather(near, "len", axis_index_groups=even)
    far = lax.all_gather(far, "len", axis_index_groups=odd)
    ext, right, left = call(
        height_kernel,
        [shaped(PLANES, EXT, LANES), shaped(GROUPS, EXT, LANES), shaped(GROUPS, EXT, LANES)],
        local + (near, far),
    )
    even_place = lax.axis_index("hgt") % 2 == 0
    near = lax.all_gather(jnp.where(even_place, right, left), "hgt", axis_index_groups=even)
    far = lax.all_gather(jnp.where(even_place, left, right), "hgt", axis_index_groups=odd)
    return call(
        main_kernel,
        shaped(1, 10, THICK, ROWS, LANES),
        (plate_state, ext, near, far),
        scratch_shapes=[
            pltpu.VMEM((FIELD_PLANES, 2, STORE, LANES), jnp.float32),
            pltpu.VMEM((THICK, 2, STORE, LANES), jnp.float32),
            pltpu.VMEM((PLANES - DISP, 2, STORE, LANES), jnp.float32),
        ],
    )


def solution(mesh):
    placed = (
        P("ply", None, None, "len", "hgt"),
        P("ply", None, "len", "hgt"),
        P("len", "hgt"),
        P("len", "hgt"),
    )
    return jax.shard_map(
        per_device,
        mesh=mesh,
        in_specs=placed,
        out_specs=P("ply", None, None, "len", "hgt"),
        check_vma=False,
    )
```

```python
import functools

import jax
import jax.numpy as jnp
from jax import lax
from jax.experimental import pallas as pl
from jax.experimental.pallas import tpu as pltpu
from jax.sharding import PartitionSpec as P

time_step = 0.25
softening = 0.15
damping = 1.0
stiffness = 2.0
pressure = 2.0

THICK = 8
ROWS = 16
LANES = 128
HALO = 8
EXT = ROWS + 2 * HALO

SCALE = 72
DISP = 80
MATE = 81
KEEP = 96
PUSH = 97
PLANES = 98
PER_GROUP = 16
GROUPS = 7

STORE = 48
TOP = 16

STRIDE = THICK + 2
VX, VY, VZ, SXX, SYY, SZZ, SXY, SXZ, SYZ = range(9)
FIELD_PLANES = 9 * STRIDE + 2

VMEM = pl.BlockSpec(memory_space=pltpu.VMEM)
PAIRS_EVEN = [[2 * i, 2 * i + 1] for i in range(8)]


def pair_groups(count, first):
    return [[(i + first) % count, (i + first + 1) % count] for i in range(0, count, 2)]


def surface_kernel(state, out):
    front = lax.axis_index("ply") == 0

    def layer(field, depth):
        return jnp.where(front, state[0, field, THICK - 1 - depth], state[0, field, depth])

    picks = [(f, 0) for f in (0, 1, 2, 9, 3, 4, 6, 7, 8)]
    picks += [(f, depth) for depth in (1, 2) for f in (7, 8, 5)]
    for k, (field, depth) in enumerate(picks):
        out[k] = layer(field, depth)


def write_tile(state, damage, frame, impact, mate, out, rows, size, front):
    for field in range(9):
        for z in range(THICK):
            out(field * THICK + z, state[0, field, z, rows, :])
    for z in range(THICK):
        out(SCALE + z, 1.0 - softening * damage[0, z, rows, :].astype(jnp.float32))
    out(DISP, jnp.where(front, state[0, 9, THICK - 1, rows, :], state[0, 9, 0, rows, :]))
    for k in range(15):
        out(MATE + k, jnp.where(front, mate[1, k, rows, :], mate[0, k, rows, :]))
    out(KEEP, (1 - frame[rows, :]).astype(jnp.float32))
    out(PUSH, impact[rows, :].astype(jnp.float32))


def length_kernel(state, damage, frame, impact, mate, near, far):
    front = lax.axis_index("ply") == 0
    core = lax.axis_index("len") % 2
    for out, start in ((near, (1 - core) * HALO), (far, core * HALO)):
        rows = pl.ds(pl.multiple_of(start, HALO), HALO)

        def put(plane, value, out=out):
            out[plane] = value

        write_tile(state, damage, frame, impact, mate, put, rows, HALO, front)


def height_kernel(state, damage, frame, impact, mate, near, far, ext, right, left):
    front = lax.axis_index("ply") == 0
    index = lax.axis_index("len")
    core = index % 2
    has_top = index > 0
    has_bottom = index < lax.axis_size("len") - 1

    def put(plane, value):
        ext[plane, HALO : HALO + ROWS, :] = value

    write_tile(state, damage, frame, impact, mate, put, slice(0, ROWS), ROWS, front)
    for plane in range(PLANES):
        top = jnp.where(core == 0, far[0, plane], near[0, plane])
        bottom = jnp.where(core == 0, near[1, plane], far[1, plane])
        ext[plane, 0:HALO, :] = jnp.where(has_top, top, 0.0)
        ext[plane, HALO + ROWS : EXT, :] = jnp.where(has_bottom, bottom, 0.0)
    slot = lax.broadcasted_iota(jnp.int32, (EXT, LANES), 1) // HALO
    for g in range(GROUPS):
        first = jnp.zeros((EXT, LANES), jnp.float32)
        last = first
        for j in range(min(PER_GROUP, PLANES - g * PER_GROUP)):
            plane = ext[g * PER_GROUP + j]
            head = pltpu.roll(plane, HALO * j, 1) if j else plane
            tail = pltpu.roll(plane, (HALO * j + HALO) % LANES, 1) if j < 15 else plane
            first = jnp.where(slot == j, head, first)
            last = jnp.where(slot == j, tail, last)
        left[g] = first
        right[g] = last


def lane_shift(x, s):
    lane = lax.broadcasted_iota(jnp.int32, x.shape, 2)
    turned = pltpu.roll(x, (-s) % LANES, 2)
    other = jnp.concatenate([turned[1:2], turned[0:1]], axis=0)
    inside = lane < LANES - s if s > 0 else lane >= -s
    return jnp.where(inside, turned, other)


def along_height(x):
    near = lane_shift(x, 1) - lane_shift(x, -1)
    return 8.0 * near - (lane_shift(x, 2) - lane_shift(x, -2))


def main_kernel(state, ext, near, far, out, fields, scale, extra):
    front = lax.axis_index("ply") == 0
    place = lax.axis_index("hgt")
    odd = place % 2
    has_left = place > 0
    has_right = place < lax.axis_size("hgt") - 1
    bonded = jnp.where(front, THICK - 1, 0)
    rows_all = slice(TOP - HALO, TOP + ROWS + HALO)

    zero = jnp.zeros((2, STORE, LANES), jnp.float32)
    for f in range(10):
        fields[f * STRIDE] = zero
        fields[f * STRIDE + 1] = zero

    lane = lax.broadcasted_iota(jnp.int32, (EXT, LANES), 1)
    is_right = (lane < HALO) & has_right
    is_left = (lane >= LANES - HALO) & has_left
    for g in range(GROUPS):
        from_right = jnp.where(odd == 0, near[1, g], far[g])
        from_left = jnp.where(odd == 0, far[g], near[0, g])
        for j in range(min(PER_GROUP, PLANES - g * PER_GROUP)):
            plane = g * PER_GROUP + j
            r = pltpu.roll(from_right, LANES - HALO * j, 1) if j else from_right
            m = pltpu.roll(from_left, LANES - HALO - HALO * j, 1) if j < 15 else from_left
            side = jnp.where(is_right, r, jnp.where(is_left, m, 0.0))
            if plane < SCALE:
                ref, at = fields, plane // THICK * STRIDE + 2 + plane % THICK
            elif plane < DISP:
                ref, at = scale, plane - SCALE
            else:
                ref, at = extra, plane - DISP
            ref[at, 0, rows_all, :] = ext[plane]
            ref[at, 1, rows_all, :] = side

    mate_at, keep_at, push_at = MATE - DISP, KEEP - DISP, PUSH - DISP
    step = time_step / 12.0

    def along_length(ref, at, r0, n):
        def tap(d):
            return ref[at, :, r0 + d : r0 + d + n, :]

        return 8.0 * (tap(1) - tap(-1)) - (tap(2) - tap(-2))

    def through(f, z, r0, n):
        def tap(d):
            return fields[f * STRIDE + 2 + z + d, :, r0 : r0 + n, :]

        return 8.0 * (tap(1) - tap(-1)) - (tap(2) - tap(-2))

    def spot(f, z):
        return f * STRIDE + 2 + z

    def velocities(r0, n, with_mate):
        keep = extra[keep_at, :, r0 : r0 + n, :]
        own = [fields[spot(f, bonded), :, r0 : r0 + n, :] for f in (VX, VY, VZ)]
        own.append(extra[0, :, r0 : r0 + n, :])
        mate = [extra[mate_at + k, :, r0 : r0 + n, :] for k in range(4)]
        pull = [
            damping * (mate[0] - own[0]),
            damping * (mate[1] - own[1]),
            stiffness * (mate[3] - own[3]) + damping * (mate[2] - own[2]),
        ]

        def body(z):
            for v, a, b, c in ((VX, SXX, SXY, SXZ), (VY, SXY, SYY, SYZ), (VZ, SXZ, SYZ, SZZ)):
                total = (
                    along_length(fields, spot(a, z), r0, n)
                    + along_height(fields[spot(b, z), :, r0 : r0 + n, :])
                    + through(c, z, r0, n)
                )
                old = fields[spot(v, z), :, r0 : r0 + n, :]
                fields[spot(v, z), :, r0 : r0 + n, :] = (old + step * total) * keep

        for z in range(THICK):
            body(z)
        for f in range(3):
            at = spot(f, bonded)
            fields[at, :, r0 : r0 + n, :] += time_step * pull[f] * keep
        push = extra[push_at, :, r0 : r0 + n, :] * keep
        at = spot(VZ, 0)
        fields[at, :, r0 : r0 + n, :] += jnp.where(front, time_step * pressure, 0.0) * push

        if with_mate:
            sign = jnp.where(front, 1.0, -1.0)
            inner = lambda k: extra[mate_at + k, :, r0 : r0 + n, :]
            fresh = []
            for f, (a, b, one, two) in enumerate(((4, 6, 9, 12), (6, 5, 10, 13), (7, 8, 11, 14))):
                total = (
                    along_length(extra, mate_at + a, r0, n)
                    + along_height(extra[mate_at + b, :, r0 : r0 + n, :])
                    + sign * (8.0 * inner(one) - inner(two))
                )
                fresh.append((mate[f] + step * total - time_step * pull[f]) * keep)
            for f in range(3):
                extra[mate_at + f, :, r0 : r0 + n, :] = fresh[f]
            extra[mate_at + 3, :, r0 : r0 + n, :] = mate[3] + time_step * fresh[2]
            extra[0, :, r0 : r0 + n, :] = (
                own[3] + time_step * fields[spot(VZ, bonded), :, r0 : r0 + n, :]
            )

    def changes(z, r0, n, size):
        def cut(x):
            return x[:size]

        def length_of(f):
            return cut(along_length(fields, spot(f, z), r0, n))

        def height_of(f):
            return cut(along_height(fields[spot(f, z), :, r0 : r0 + n, :]))

        def depth_of(f):
            return cut(through(f, z, r0, n))

        factor = step * scale[z, 0:size, r0 : r0 + n, :]
        xx, yy, zz = length_of(VX), height_of(VY), depth_of(VZ)
        whole = xx + yy + zz
        return (
            factor * (whole + 2.0 * xx),
            factor * (whole + 2.0 * yy),
            factor * (whole + 2.0 * zz),
            factor * (height_of(VX) + length_of(VY)),
            factor * (depth_of(VX) + length_of(VZ)),
            factor * (depth_of(VY) + height_of(VZ)),
        )

    velocities(TOP - HALO, EXT, True)

    def first_stress(z):
        r0, n = TOP - 4, ROWS + 8
        for f, change in enumerate(changes(z, r0, n, 2)):
            fields[spot(SXX + f, z), :, r0 : r0 + n, :] += change
        out[0, 9, z] = state[0, 9, z] + time_step * fields[spot(VZ, z), 0, TOP : TOP + ROWS, :]

    for z in range(THICK):
        first_stress(z)
    velocities(TOP - 4, ROWS + 8, False)

    def last_stress(z):
        for f in range(3):
            out[0, f, z] = fields[spot(f, z), 0, TOP : TOP + ROWS, :]
        for f, change in enumerate(changes(z, TOP, ROWS, 1)):
            out[0, 3 + f, z] = fields[spot(SXX + f, z), 0, TOP : TOP + ROWS, :] + change[0]
        out[0, 9, z] += time_step * fields[spot(VZ, z), 0, TOP : TOP + ROWS, :]

    for z in range(THICK):
        last_stress(z)


def shaped(*shape):
    return jax.ShapeDtypeStruct(shape, jnp.float32)


def call(kernel, outs, args, **more):
    return pl.pallas_call(
        kernel,
        out_shape=outs,
        in_specs=[VMEM] * len(args),
        out_specs=jax.tree.map(lambda _: VMEM, outs),
        compiler_params=pltpu.CompilerParams(vmem_limit_bytes=32 * 2**20),
        **more,
    )(*args)


def per_device(plate_state, damage, frame_mask, impact_mask):
    even, odd = pair_groups(16, 0), pair_groups(16, 1)
    surface = call(surface_kernel, shaped(15, ROWS, LANES), (plate_state,))
    mate = lax.all_gather(surface, "ply")
    local = (plate_state, damage, frame_mask, impact_mask, mate)
    near, far = call(length_kernel, [shaped(PLANES, HALO, LANES)] * 2, local)
    near = lax.all_gather(near, "len", axis_index_groups=even)
    far = lax.all_gather(far, "len", axis_index_groups=odd)
    ext, right, left = call(
        height_kernel,
        [shaped(PLANES, EXT, LANES), shaped(GROUPS, EXT, LANES), shaped(GROUPS, EXT, LANES)],
        local + (near, far),
    )
    even_place = lax.axis_index("hgt") % 2 == 0
    swap = [(i, j) for pair in odd[:-1] for i, j in (pair, pair[::-1])]
    far = lax.ppermute(jnp.where(even_place, left, right), "hgt", swap)
    near = lax.all_gather(jnp.where(even_place, right, left), "hgt", axis_index_groups=even)
    return call(
        main_kernel,
        shaped(1, 10, THICK, ROWS, LANES),
        (plate_state, ext, near, far),
        scratch_shapes=[
            pltpu.VMEM((FIELD_PLANES, 2, STORE, LANES), jnp.float32),
            pltpu.VMEM((THICK, 2, STORE, LANES), jnp.float32),
            pltpu.VMEM((PLANES - DISP, 2, STORE, LANES), jnp.float32),
        ],
    )


def solution(mesh):
    placed = (
        P("ply", None, None, "len", "hgt"),
        P("ply", None, "len", "hgt"),
        P("len", "hgt"),
        P("len", "hgt"),
    )
    return jax.shard_map(
        per_device,
        mesh=mesh,
        in_specs=placed,
        out_specs=P("ply", None, None, "len", "hgt"),
        check_vma=False,
    )
```

```python
import jax
import jax.numpy as jnp
from jax import lax
from jax.experimental import pallas as pl
from jax.experimental.pallas import tpu as pltpu
from jax.sharding import PartitionSpec as P

time_step = 0.25
softening = 0.15
damping = 1.0
stiffness = 2.0
pressure = 2.0

THICK = 8
ROWS = 16
LANES = 128
HALO = 8
STEP = time_step / 12.0

VX, VY, VZ, SXX, SYY, SZZ, SXY, SXZ, SYZ, SCALE = range(10)
DISP, KEEP, PUSH, OWN = 80, 81, 82, 83
DISP_ALL = 83
MATE = 83
ALL = 98
M_VX, M_VY, M_VZ, M_W, M_XX, M_YY, M_XY, M_XZ, M_YZ = range(MATE, MATE + 9)
M_XZ1, M_YZ1, M_ZZ1, M_XZ2, M_YZ2, M_ZZ2 = range(MATE + 9, MATE + 15)

PER_GROUP = 16
GROUPS = 6
MATE_SENT = 17

VMEM = pl.BlockSpec(memory_space=pltpu.VMEM)
MIB = 2**20


def at(field, z):
    return field * THICK + z


def fours():
    items = [(at(f, z), False) for f in (SXX, SXY, SXZ, SCALE) for z in range(THICK)]
    items += [(at(f, z), True) for f in (VX, VY, VZ) for z in range(THICK)]
    return items + [(p, False) for p in (M_XX, M_XY, M_XZ)]


def twos():
    items = [at(f, z) for f in (SYY, SZZ, SYZ, VX, VY, VZ) for z in range(THICK)]
    items += [M_VX, M_VY, M_VZ, M_W, M_YY, M_YZ, M_XZ1, M_YZ1, M_ZZ1, M_XZ2, M_YZ2, M_ZZ2]
    return items + [DISP, KEEP, PUSH]


def travel(down):
    moves, row = [], 0
    for plane, new in fours():
        first = (10 if new else 12) if down else (2 if new else 0)
        moves.append((plane, first, 4, new, row // 8, row % 8))
        row += 4
    for plane in twos():
        moves.append((plane, 14 if down else 0, 2, False, row // 8, row % 8))
        row += 2
    return moves


SENT = -(-(4 * len(fours()) + 2 * len(twos())) // 8)
SENT_SIDES = -(-SENT // 8)
SENT_ALL = SENT + SENT_SIDES


def lanes_of(rows):
    return lax.broadcasted_iota(jnp.int32, (rows, LANES), 1)


def turn(x, by):
    by %= LANES
    return pltpu.roll(x, by, 1) if by else x


def pack_sides(planes):
    slot = lanes_of(planes[0].shape[0]) // 16
    packed = jnp.zeros(planes[0].shape, jnp.float32)
    for j, plane in enumerate(planes):
        packed = jnp.where(slot == j, turn(plane, HALO + 16 * j), packed)
    return packed


def unpack_side(packed, j):
    lane = lanes_of(packed.shape[0])
    side = turn(packed, -(HALO + 16 * j))
    return jnp.where((lane < HALO) | (lane >= LANES - HALO), side, 0.0)


def lane_shift(x, s):
    lane = lax.broadcasted_iota(jnp.int32, x.shape, 2)
    turned = pltpu.roll(x, (-s) % LANES, 2)
    other = jnp.concatenate([turned[1:2], turned[0:1]], axis=0)
    inside = lane < LANES - s if s > 0 else lane >= -s
    return jnp.where(inside, turned, other)


def along_height(x):
    near = lane_shift(x, 1) - lane_shift(x, -1)
    return 8.0 * near - (lane_shift(x, 2) - lane_shift(x, -2))


def along_length(look, plane, r0, n):
    near = look(plane, r0 + 1, n) - look(plane, r0 - 1, n)
    return 8.0 * near - (look(plane, r0 + 2, n) - look(plane, r0 - 2, n))


def through(look, field, z, r0, n):
    def layer(k):
        return look(at(field, k), r0, n) if 0 <= k < THICK else jnp.zeros((2, n, LANES), jnp.float32)

    return 8.0 * (layer(z + 1) - layer(z - 1)) - (layer(z + 2) - layer(z - 2))


def new_velocities(look, r0, n, front, put, with_mate):
    keep = look(KEEP, r0, n)

    def bonded(field):
        return jnp.where(front, look(at(field, THICK - 1), r0, n), look(at(field, 0), r0, n))

    mate = [look(p, r0, n) for p in (M_VX, M_VY, M_VZ, M_W)]
    pull = [
        damping * (mate[0] - bonded(VX)),
        damping * (mate[1] - bonded(VY)),
        stiffness * (mate[3] - look(DISP, r0, n)) + damping * (mate[2] - bonded(VZ)),
    ]
    pull = [time_step * p for p in pull]
    push = jnp.where(front, time_step * pressure, 0.0) * look(PUSH, r0, n)
    if with_mate:
        sign = jnp.where(front, 1.0, -1.0)
        parts = ((M_XX, M_XY, M_XZ1, M_XZ2), (M_XY, M_YY, M_YZ1, M_YZ2), (M_XZ, M_YZ, M_ZZ1, M_ZZ2))
        for f, (a, b, one, two) in enumerate(parts):
            total = (
                along_length(look, a, r0, n)
                + along_height(look(b, r0, n))
                + sign * (8.0 * look(one, r0, n) - look(two, r0, n))
            )
            put(M_VX + f, (mate[f] + STEP * total - pull[f]) * keep)
    for z in range(THICK):
        for f, (a, b, c) in enumerate(((SXX, SXY, SXZ), (SXY, SYY, SYZ), (SXZ, SYZ, SZZ))):
            total = (
                along_length(look, at(a, z), r0, n)
                + along_height(look(at(b, z), r0, n))
                + through(look, c, z, r0, n)
            )
            fresh = look(at(f, z), r0, n) + STEP * total
            if z == 0:
                fresh += jnp.where(front, 0.0, 1.0) * pull[f]
                if f == 2:
                    fresh += push
            if z == THICK - 1:
                fresh += jnp.where(front, 1.0, 0.0) * pull[f]
            put(at(f, z), fresh * keep)


def fetch_kernel(state, damage, frame, impact, tile, near, far, levels, held, struck, arrived):
    copies = [
        pltpu.make_async_copy(damage.at[0], levels, arrived.at[10]),
        pltpu.make_async_copy(frame, held, arrived.at[11]),
        pltpu.make_async_copy(impact, struck, arrived.at[12]),
    ]
    for f in range(10):
        first = DISP_ALL if f == 9 else at(f, 0)
        copies.append(
            pltpu.make_async_copy(state.at[0, f], tile.at[pl.ds(first, THICK)], arrived.at[f])
        )
    for copy in copies:
        copy.start()
    for copy in copies:
        copy.wait()
    front = lax.axis_index("ply") == 0
    even = lax.axis_index("hgt") % 2 == 0
    for z in range(THICK):
        tile[at(SCALE, z)] = 1.0 - softening * levels[z].astype(jnp.float32)
    tile[DISP] = jnp.where(front, tile[DISP_ALL + THICK - 1], tile[DISP_ALL])
    tile[KEEP] = (1 - held[...]).astype(jnp.float32)
    tile[PUSH] = struck[...].astype(jnp.float32)
    slot = lanes_of(ROWS) // HALO
    for g in range(GROUPS):
        first = jnp.zeros((ROWS, LANES), jnp.float32)
        last = first
        for j in range(min(PER_GROUP, OWN - g * PER_GROUP)):
            plane = tile[g * PER_GROUP + j]
            first = jnp.where(slot == j, turn(plane, HALO * j), first)
            last = jnp.where(slot == j, turn(plane, HALO * j + HALO), last)
        near[g] = jnp.where(even, last, first)
        far[g] = jnp.where(even, first, last)


def side_kernel(tile, near, far, side, surface):
    front = lax.axis_index("ply") == 0
    place = lax.axis_index("hgt")
    even = place % 2 == 0
    lane = lanes_of(ROWS)
    is_right = (lane < HALO) & (place < lax.axis_size("hgt") - 1)
    is_left = (lane >= LANES - HALO) & (place > 0)
    for g in range(GROUPS):
        from_right = jnp.where(even, near[1, g], far[g])
        from_left = jnp.where(even, far[g], near[0, g])
        for j in range(min(PER_GROUP, OWN - g * PER_GROUP)):
            r = turn(from_right, -HALO * j)
            m = turn(from_left, -HALO - HALO * j)
            side[g * PER_GROUP + j] = jnp.where(is_right, r, jnp.where(is_left, m, 0.0))
    picks = [(VX, 0), (VY, 0), (VZ, 0), None, (SXX, 0), (SYY, 0), (SXY, 0), (SXZ, 0), (SYZ, 0)]
    picks += [(f, depth) for depth in (1, 2) for f in (SXZ, SYZ, SZZ)]
    sides = []
    for k, pick in enumerate(picks):
        if pick is None:
            surface[k] = tile[DISP]
            sides.append(side[DISP])
        else:
            low, high = at(pick[0], pick[1]), at(pick[0], THICK - 1 - pick[1])
            surface[k] = jnp.where(front, tile[high], tile[low])
            sides.append(jnp.where(front, side[high], side[low]))
    surface[15] = pack_sides(sides[:8])
    surface[16] = pack_sides(sides[8:])


def speed_kernel(tile, side, mates, fresh, mate, near, far, middle, flank):
    front = lax.axis_index("ply") == 0
    core = lax.axis_index("len") % 2
    other = jnp.where(front, 1, 0)
    for k in range(15):
        mate[k, 0] = mates[other, k]
        mate[k, 1] = unpack_side(mates[other, 15 + k // 8], k % 8)

    def look(plane, r, n):
        if plane >= MATE:
            return mate[plane - MATE, :, r : r + n, :]
        return jnp.stack([tile[plane, r : r + n, :], side[plane, r : r + n, :]])

    def put(plane, value):
        fresh[plane if plane < 24 else 24 + plane - MATE, :, 2 : ROWS - 2, :] = value

    new_velocities(look, 2, ROWS - 4, front, put, True)

    for down in (0, 1):
        middle[down, SENT - 1] = jnp.zeros((HALO, LANES), jnp.float32)
        flank[down, SENT - 1] = jnp.zeros((HALO, LANES), jnp.float32)
        for plane, r, n, new, k, row in travel(down):
            value = fresh[plane, :, r : r + n, :] if new else look(plane, r, n)
            middle[down, k, row : row + n, :] = value[0]
            flank[down, k, row : row + n, :] = value[1]
    for out, way in ((near, 1 - core), (far, core)):
        for k in range(SENT):
            out[k] = middle[way, k]
        for g in range(SENT_SIDES):
            ks = range(8 * g, min(8 * g + 8, SENT))
            out[SENT + g] = pack_sides([flank[way, k] for k in ks])


def last_kernel(tile, side, fresh, mate, near, far, out, cells):
    front = lax.axis_index("ply") == 0
    index = lax.axis_index("len")
    upper = index % 2 == 0
    has_top = index > 0
    has_bottom = index < lax.axis_size("len") - 1

    for plane in range(OWN):
        cells[plane, 0, HALO : HALO + ROWS, :] = tile[plane]
        cells[plane, 1, HALO : HALO + ROWS, :] = side[plane]
    for k in range(15):
        cells[MATE + k, :, HALO : HALO + ROWS, :] = mate[k]
    for k in range(27):
        plane = k if k < 24 else MATE + k - 24
        cells[plane, :, HALO + 2 : HALO + ROWS - 2, :] = fresh[k, :, 2 : ROWS - 2, :]
    for down, there in ((1, has_top), (0, has_bottom)):

        def sent(k):
            first, second = (far[0, k], near[0, k]) if down else (near[1, k], far[1, k])
            return jnp.where(there, jnp.where(upper, first, second), 0.0)

        packed = [sent(SENT + g) for g in range(SENT_SIDES)]
        move = -ROWS if down else ROWS
        held = None
        for plane, r, n, _, k, row in travel(down):
            if k != held:
                held, main, flank = k, sent(k), unpack_side(packed[k // 8], k % 8)
            place = HALO + r + move
            cells[plane, 0, place : place + n, :] = main[row : row + n]
            cells[plane, 1, place : place + n, :] = flank[row : row + n]

    def look(plane, r, n):
        return cells[plane, :, HALO + r : HALO + r + n, :]

    def writer(r, n):
        def put(plane, value):
            cells[plane, :, HALO + r : HALO + r + n, :] = value

        return put

    for r in (-2, ROWS - 2):
        new_velocities(look, r, 4, front, writer(r, 4), True)
    r, n = -2, ROWS + 4
    put = writer(r, n)
    own_z = jnp.where(front, look(at(VZ, THICK - 1), r, n), look(at(VZ, 0), r, n))
    put(DISP, look(DISP, r, n) + time_step * own_z)
    put(M_W, look(M_W, r, n) + time_step * look(M_VZ, r, n))

    def changes(z, r, n, size):
        def length_of(f):
            return along_length(look, at(f, z), r, n)[:size]

        def height_of(f):
            return along_height(look(at(f, z), r, n))[:size]

        def depth_of(f):
            return through(look, f, z, r, n)[:size]

        factor = STEP * look(at(SCALE, z), r, n)[:size]
        xx, yy, zz = length_of(VX), height_of(VY), depth_of(VZ)
        whole = xx + yy + zz
        return (
            factor * (whole + 2.0 * xx),
            factor * (whole + 2.0 * yy),
            factor * (whole + 2.0 * zz),
            factor * (height_of(VX) + length_of(VY)),
            factor * (depth_of(VX) + length_of(VZ)),
            factor * (depth_of(VY) + height_of(VZ)),
        )

    r, n = -4, ROWS + 8
    put = writer(r, n)
    for z in range(THICK):
        for f, change in enumerate(changes(z, r, n, 2)):
            put(at(SXX + f, z), look(at(SXX + f, z), r, n) + change)
        out[0, 9, z] = tile[DISP_ALL + z] + time_step * look(at(VZ, z), 0, ROWS)[0]
    new_velocities(look, -2, ROWS + 4, front, writer(-2, ROWS + 4), False)
    for z in range(THICK):
        for f in range(3):
            out[0, f, z] = look(at(f, z), 0, ROWS)[0]
        for f, change in enumerate(changes(z, 0, ROWS, 1)):
            out[0, 3 + f, z] = look(at(SXX + f, z), 0, ROWS)[0] + change[0]
        out[0, 9, z] += time_step * look(at(VZ, z), 0, ROWS)[0]


def shaped(*shape):
    return jax.ShapeDtypeStruct(shape, jnp.float32)


def call(kernel, outs, args, limit=32 * MIB, space=pltpu.VMEM, scratch=()):
    return pl.pallas_call(
        kernel,
        out_shape=outs,
        in_specs=[pl.BlockSpec(memory_space=space)] * len(args),
        out_specs=jax.tree.map(lambda _: VMEM, outs),
        scratch_shapes=scratch,
        compiler_params=pltpu.CompilerParams(vmem_limit_bytes=limit),
    )(*args)


FETCH_LIMIT = 32 * MIB


def per_device(plate_state, damage, frame_mask, impact_mask):
    even = [[2 * i, 2 * i + 1] for i in range(8)]
    odd = [[2 * i + 1, (2 * i + 2) % 16] for i in range(8)]
    strips = shaped(GROUPS, ROWS, LANES)
    tile, near, far = call(
        fetch_kernel,
        [shaped(OWN + THICK, ROWS, LANES), strips, strips],
        (plate_state, damage, frame_mask, impact_mask),
        limit=FETCH_LIMIT,
        space=pl.ANY,
        scratch=[
            pltpu.VMEM((THICK, ROWS, LANES), jnp.int32),
            pltpu.VMEM((ROWS, LANES), jnp.int32),
            pltpu.VMEM((ROWS, LANES), jnp.int32),
            pltpu.SemaphoreType.DMA((13,)),
        ],
    )
    swap = [(i, j) for pair in odd[:-1] for i, j in (pair, pair[::-1])]
    far = lax.ppermute(far, "hgt", swap)
    near = lax.all_gather(near, "hgt", axis_index_groups=even)
    side, surface = call(
        side_kernel,
        [shaped(OWN, ROWS, LANES), shaped(MATE_SENT, ROWS, LANES)],
        (tile, near, far),
    )
    mates = lax.all_gather(surface, "ply")
    sent = shaped(SENT_ALL, HALO, LANES)
    fresh, mate, near, far = call(
        speed_kernel,
        [shaped(27, 2, ROWS, LANES), shaped(15, 2, ROWS, LANES), sent, sent],
        (tile, side, mates),
        scratch=[pltpu.VMEM((2, SENT, HALO, LANES), jnp.float32)] * 2,
    )
    near = lax.all_gather(near, "len", axis_index_groups=even)
    far = lax.all_gather(far, "len", axis_index_groups=odd)
    return call(
        last_kernel,
        shaped(1, 10, THICK, ROWS, LANES),
        (tile, side, fresh, mate, near, far),
        scratch=[pltpu.VMEM((ALL, 2, ROWS + 2 * HALO, LANES), jnp.float32)],
    )


def solution(mesh):
    placed = (
        P("ply", None, None, "len", "hgt"),
        P("ply", None, "len", "hgt"),
        P("len", "hgt"),
        P("len", "hgt"),
    )
    return jax.shard_map(
        per_device,
        mesh=mesh,
        in_specs=placed,
        out_specs=P("ply", None, None, "len", "hgt"),
        check_vma=False,
    )
```

```python
import jax
import jax.numpy as jnp
from jax import lax
from jax.experimental import pallas as pl
from jax.experimental.pallas import tpu as pltpu
from jax.sharding import PartitionSpec as P

time_step = 0.25
softening = 0.15
damping = 1.0
stiffness = 2.0
pressure = 2.0

THICK = 8
ROWS = 16
LANES = 128
HALO = 8
STEP = time_step / 12.0

VX, VY, VZ, SXX, SYY, SZZ, SXY, SXZ, SYZ, SCALE = range(10)
DISP, KEEP, PUSH, OWN = 80, 81, 82, 83
SPARE = 83
MATE = 83
ALL = 98
M_VX, M_VY, M_VZ, M_W, M_XX, M_YY, M_XY, M_XZ, M_YZ = range(MATE, MATE + 9)
M_XZ1, M_YZ1, M_ZZ1, M_XZ2, M_YZ2, M_ZZ2 = range(MATE + 9, MATE + 15)

PICKS = [(VX, 0), (VY, 0), (VZ, 0), None, (SXX, 0), (SYY, 0), (SXY, 0), (SXZ, 0), (SYZ, 0)]
PICKS += [(f, depth) for depth in (1, 2) for f in (SXZ, SYZ, SZZ)]

PER_GROUP = 16
GROUPS = 6
MATE_SENT = 17

VMEM = pl.BlockSpec(memory_space=pltpu.VMEM)
MIB = 2**20


def at(field, z):
    return field * THICK + z


def fours():
    items = [(at(f, z), False) for f in (SXX, SXY, SXZ, SCALE) for z in range(THICK)]
    items += [(at(f, z), True) for f in (VX, VY, VZ) for z in range(THICK)]
    return items + [(p, False) for p in (M_XX, M_XY, M_XZ)]


def twos():
    items = [at(f, z) for f in (SYY, SZZ, SYZ, VX, VY, VZ) for z in range(THICK)]
    items += [M_VX, M_VY, M_VZ, M_W, M_YY, M_YZ, M_XZ1, M_YZ1, M_ZZ1, M_XZ2, M_YZ2, M_ZZ2]
    return items + [DISP, KEEP, PUSH]


def travel(down):
    moves, row = [], 0
    for plane, new in fours():
        first = (10 if new else 12) if down else (2 if new else 0)
        moves.append((plane, first, 4, new, row // 8, row % 8))
        row += 4
    for plane in twos():
        moves.append((plane, 14 if down else 0, 2, False, row // 8, row % 8))
        row += 2
    return moves


SENT = -(-(4 * len(fours()) + 2 * len(twos())) // 8)
SENT_SIDES = -(-SENT // 8)
SENT_ALL = SENT + SENT_SIDES


def lanes_of(rows):
    return lax.broadcasted_iota(jnp.int32, (rows, LANES), 1)


def turn(x, by):
    by %= LANES
    return pltpu.roll(x, by, 1) if by else x


def pack_sides(planes):
    slot = lanes_of(planes[0].shape[0]) // 16
    packed = jnp.zeros(planes[0].shape, jnp.float32)
    for j, plane in enumerate(planes):
        packed = jnp.where(slot == j, turn(plane, HALO + 16 * j), packed)
    return packed


def unpack_side(packed, j):
    lane = lanes_of(packed.shape[0])
    side = turn(packed, -(HALO + 16 * j))
    return jnp.where((lane < HALO) | (lane >= LANES - HALO), side, 0.0)


def lane_shift(x, s):
    lane = lax.broadcasted_iota(jnp.int32, x.shape, 2)
    turned = pltpu.roll(x, (-s) % LANES, 2)
    other = jnp.concatenate([turned[1:2], turned[0:1]], axis=0)
    inside = lane < LANES - s if s > 0 else lane >= -s
    return jnp.where(inside, turned, other)


def along_height(x):
    near = lane_shift(x, 1) - lane_shift(x, -1)
    return 8.0 * near - (lane_shift(x, 2) - lane_shift(x, -2))


def along_length(look, plane, r0, n):
    near = look(plane, r0 + 1, n) - look(plane, r0 - 1, n)
    return 8.0 * near - (look(plane, r0 + 2, n) - look(plane, r0 - 2, n))


def through(look, field, z, r0, n):
    def layer(k):
        return look(at(field, k), r0, n) if 0 <= k < THICK else jnp.zeros((2, n, LANES), jnp.float32)

    return 8.0 * (layer(z + 1) - layer(z - 1)) - (layer(z + 2) - layer(z - 2))


def new_velocities(look, r0, n, front, put, with_mate):
    keep = look(KEEP, r0, n)

    def bonded(field):
        return jnp.where(front, look(at(field, THICK - 1), r0, n), look(at(field, 0), r0, n))

    mate = [look(p, r0, n) for p in (M_VX, M_VY, M_VZ, M_W)]
    pull = [
        damping * (mate[0] - bonded(VX)),
        damping * (mate[1] - bonded(VY)),
        stiffness * (mate[3] - look(DISP, r0, n)) + damping * (mate[2] - bonded(VZ)),
    ]
    pull = [time_step * p for p in pull]
    push = jnp.where(front, time_step * pressure, 0.0) * look(PUSH, r0, n)
    if with_mate:
        sign = jnp.where(front, 1.0, -1.0)
        parts = ((M_XX, M_XY, M_XZ1, M_XZ2), (M_XY, M_YY, M_YZ1, M_YZ2), (M_XZ, M_YZ, M_ZZ1, M_ZZ2))
        for f, (a, b, one, two) in enumerate(parts):
            total = (
                along_length(look, a, r0, n)
                + along_height(look(b, r0, n))
                + sign * (8.0 * look(one, r0, n) - look(two, r0, n))
            )
            put(M_VX + f, (mate[f] + STEP * total - pull[f]) * keep)
    for z in range(THICK):
        for f, (a, b, c) in enumerate(((SXX, SXY, SXZ), (SXY, SYY, SYZ), (SXZ, SYZ, SZZ))):
            total = (
                along_length(look, at(a, z), r0, n)
                + along_height(look(at(b, z), r0, n))
                + through(look, c, z, r0, n)
            )
            fresh = look(at(f, z), r0, n) + STEP * total
            if z == 0:
                fresh += jnp.where(front, 0.0, 1.0) * pull[f]
                if f == 2:
                    fresh += push
            if z == THICK - 1:
                fresh += jnp.where(front, 1.0, 0.0) * pull[f]
            put(at(f, z), fresh * keep)


def fetch_kernel(state, damage, frame, impact, near, far, surface, tile, levels, held, struck, arrived):
    copies = [
        pltpu.make_async_copy(damage.at[0], levels, arrived.at[10]),
        pltpu.make_async_copy(frame, held, arrived.at[11]),
        pltpu.make_async_copy(impact, struck, arrived.at[12]),
    ]
    for f in range(10):
        first = SPARE if f == 9 else at(f, 0)
        copies.append(
            pltpu.make_async_copy(state.at[0, f], tile.at[pl.ds(first, THICK)], arrived.at[f])
        )
    for copy in copies:
        copy.start()
    for copy in copies:
        copy.wait()
    front = lax.axis_index("ply") == 0
    even = lax.axis_index("hgt") % 2 == 0
    for z in range(THICK):
        tile[at(SCALE, z)] = 1.0 - softening * levels[z].astype(jnp.float32)
    tile[DISP] = jnp.where(front, tile[SPARE + THICK - 1], tile[SPARE])
    tile[KEEP] = (1 - held[...]).astype(jnp.float32)
    tile[PUSH] = struck[...].astype(jnp.float32)
    slot = lanes_of(ROWS) // HALO
    for g in range(GROUPS):
        first = jnp.zeros((ROWS, LANES), jnp.float32)
        last = first
        for j in range(min(PER_GROUP, OWN - g * PER_GROUP)):
            plane = tile[g * PER_GROUP + j]
            first = jnp.where(slot == j, turn(plane, HALO * j), first)
            last = jnp.where(slot == j, turn(plane, HALO * j + HALO), last)
        near[g] = jnp.where(even, last, first)
        far[g] = jnp.where(even, first, last)
    for k, pick in enumerate(PICKS):
        if pick is None:
            surface[k] = tile[DISP]
        else:
            low, high = at(pick[0], pick[1]), at(pick[0], THICK - 1 - pick[1])
            surface[k] = jnp.where(front, tile[high], tile[low])


def side_kernel(own, near, far, side, surface):
    front = lax.axis_index("ply") == 0
    place = lax.axis_index("hgt")
    even = place % 2 == 0
    lane = lanes_of(ROWS)
    is_right = (lane < HALO) & (place < lax.axis_size("hgt") - 1)
    is_left = (lane >= LANES - HALO) & (place > 0)
    for g in range(GROUPS):
        from_right = jnp.where(even, near[1, g], far[g])
        from_left = jnp.where(even, far[g], near[0, g])
        for j in range(min(PER_GROUP, OWN - g * PER_GROUP)):
            r = turn(from_right, -HALO * j)
            m = turn(from_left, -HALO - HALO * j)
            side[g * PER_GROUP + j] = jnp.where(is_right, r, jnp.where(is_left, m, 0.0))
    sides = []
    for k, pick in enumerate(PICKS):
        surface[k] = own[k]
        if pick is None:
            sides.append(side[DISP])
        else:
            low, high = at(pick[0], pick[1]), at(pick[0], THICK - 1 - pick[1])
            sides.append(jnp.where(front, side[high], side[low]))
    surface[15] = pack_sides(sides[:8])
    surface[16] = pack_sides(sides[8:])


def speed_kernel(
    state, damage, frame, impact, side, mates, fresh, mate, extra, near, far, middle, flank
):
    front = lax.axis_index("ply") == 0
    for z in range(THICK):
        extra[z] = 1.0 - softening * damage[0, z].astype(jnp.float32)
    extra[DISP - 72] = jnp.where(front, state[0, 9, THICK - 1], state[0, 9, 0])
    extra[KEEP - 72] = (1 - frame[...]).astype(jnp.float32)
    extra[PUSH - 72] = impact[...].astype(jnp.float32)
    core = lax.axis_index("len") % 2
    other = jnp.where(front, 1, 0)
    for k in range(15):
        mate[k, 0] = mates[other, k]
        mate[k, 1] = unpack_side(mates[other, 15 + k // 8], k % 8)

    def look(plane, r, n):
        if plane >= MATE:
            return mate[plane - MATE, :, r : r + n, :]
        if plane >= 72:
            main = extra[plane - 72, r : r + n, :]
        else:
            main = state[0, plane // THICK, plane % THICK, r : r + n, :]
        return jnp.stack([main, side[plane, r : r + n, :]])

    def put(plane, value):
        fresh[plane if plane < 24 else 24 + plane - MATE, :, 2 : ROWS - 2, :] = value

    new_velocities(look, 2, ROWS - 4, front, put, True)

    for down in (0, 1):
        middle[down, SENT - 1] = jnp.zeros((HALO, LANES), jnp.float32)
        flank[down, SENT - 1] = jnp.zeros((HALO, LANES), jnp.float32)
        for plane, r, n, new, k, row in travel(down):
            value = fresh[plane, :, r : r + n, :] if new else look(plane, r, n)
            middle[down, k, row : row + n, :] = value[0]
            flank[down, k, row : row + n, :] = value[1]
    for out, way in ((near, 1 - core), (far, core)):
        for k in range(SENT):
            out[k] = middle[way, k]
        for g in range(SENT_SIDES):
            ks = range(8 * g, min(8 * g + 8, SENT))
            out[SENT + g] = pack_sides([flank[way, k] for k in ks])


def last_kernel(state, extra, side, fresh, mate, near, far, out, cells):
    front = lax.axis_index("ply") == 0
    index = lax.axis_index("len")
    upper = index % 2 == 0
    has_top = index > 0
    has_bottom = index < lax.axis_size("len") - 1

    for plane in range(OWN):
        if plane >= 72:
            main = extra[plane - 72]
        else:
            main = state[0, plane // THICK, plane % THICK]
        cells[plane, 0, HALO : HALO + ROWS, :] = main
        cells[plane, 1, HALO : HALO + ROWS, :] = side[plane]
    for k in range(15):
        cells[MATE + k, :, HALO : HALO + ROWS, :] = mate[k]
    for k in range(27):
        plane = k if k < 24 else MATE + k - 24
        cells[plane, :, HALO + 2 : HALO + ROWS - 2, :] = fresh[k, :, 2 : ROWS - 2, :]
    for down, there in ((1, has_top), (0, has_bottom)):

        def sent(k):
            first, second = (far[k], near[0, k]) if down else (near[1, k], far[k])
            return jnp.where(there, jnp.where(upper, first, second), 0.0)

        packed = [sent(SENT + g) for g in range(SENT_SIDES)]
        move = -ROWS if down else ROWS
        held = None
        for plane, r, n, _, k, row in travel(down):
            if k != held:
                held, main, flank = k, sent(k), unpack_side(packed[k // 8], k % 8)
            place = HALO + r + move
            cells[plane, 0, place : place + n, :] = main[row : row + n]
            cells[plane, 1, place : place + n, :] = flank[row : row + n]

    def look(plane, r, n):
        return cells[plane, :, HALO + r : HALO + r + n, :]

    def writer(r, n):
        def put(plane, value):
            cells[plane, :, HALO + r : HALO + r + n, :] = value

        return put

    for r in (-2, ROWS - 2):
        new_velocities(look, r, 4, front, writer(r, 4), True)
    r, n = -2, ROWS + 4
    put = writer(r, n)
    own_z = jnp.where(front, look(at(VZ, THICK - 1), r, n), look(at(VZ, 0), r, n))
    put(DISP, look(DISP, r, n) + time_step * own_z)
    put(M_W, look(M_W, r, n) + time_step * look(M_VZ, r, n))

    def changes(z, r, n, size):
        def length_of(f):
            return along_length(look, at(f, z), r, n)[:size]

        def height_of(f):
            return along_height(look(at(f, z), r, n))[:size]

        def depth_of(f):
            return through(look, f, z, r, n)[:size]

        factor = STEP * look(at(SCALE, z), r, n)[:size]
        xx, yy, zz = length_of(VX), height_of(VY), depth_of(VZ)
        whole = xx + yy + zz
        return (
            factor * (whole + 2.0 * xx),
            factor * (whole + 2.0 * yy),
            factor * (whole + 2.0 * zz),
            factor * (height_of(VX) + length_of(VY)),
            factor * (depth_of(VX) + length_of(VZ)),
            factor * (depth_of(VY) + height_of(VZ)),
        )

    r, n = -4, ROWS + 8
    put = writer(r, n)
    for z in range(THICK):
        for f, change in enumerate(changes(z, r, n, 2)):
            put(at(SXX + f, z), look(at(SXX + f, z), r, n) + change)
        out[0, 9, z] = state[0, 9, z] + time_step * look(at(VZ, z), 0, ROWS)[0]
    new_velocities(look, -2, ROWS + 4, front, writer(-2, ROWS + 4), False)
    for z in range(THICK):
        for f in range(3):
            out[0, f, z] = look(at(f, z), 0, ROWS)[0]
        for f, change in enumerate(changes(z, 0, ROWS, 1)):
            out[0, 3 + f, z] = look(at(SXX + f, z), 0, ROWS)[0] + change[0]
        out[0, 9, z] += time_step * look(at(VZ, z), 0, ROWS)[0]


def shaped(*shape):
    return jax.ShapeDtypeStruct(shape, jnp.float32)


def call(kernel, outs, args, limit=32 * MIB, space=pltpu.VMEM, scratch=()):
    return pl.pallas_call(
        kernel,
        out_shape=outs,
        in_specs=[pl.BlockSpec(memory_space=space)] * len(args),
        out_specs=jax.tree.map(lambda _: VMEM, outs),
        scratch_shapes=scratch,
        compiler_params=pltpu.CompilerParams(vmem_limit_bytes=limit),
    )(*args)


FETCH_LIMIT = 60 * MIB


def per_device(plate_state, damage, frame_mask, impact_mask):
    even = [[2 * i, 2 * i + 1] for i in range(8)]
    odd = [[2 * i + 1, (2 * i + 2) % 16] for i in range(8)]
    strips = shaped(GROUPS, ROWS, LANES)
    near, far, surface = call(
        fetch_kernel,
        [strips, strips, shaped(15, ROWS, LANES)],
        (plate_state, damage, frame_mask, impact_mask),
        limit=FETCH_LIMIT,
        space=pl.ANY,
        scratch=[
            pltpu.VMEM((OWN + THICK, ROWS, LANES), jnp.float32),
            pltpu.VMEM((THICK, ROWS, LANES), jnp.int32),
            pltpu.VMEM((ROWS, LANES), jnp.int32),
            pltpu.VMEM((ROWS, LANES), jnp.int32),
            pltpu.SemaphoreType.DMA((13,)),
        ],
    )
    swap = [(i, j) for pair in odd[:-1] for i, j in (pair, pair[::-1])]
    far = lax.ppermute(far, "hgt", swap)
    near = lax.all_gather(near, "hgt", axis_index_groups=even)
    side, surface = call(
        side_kernel,
        [shaped(OWN, ROWS, LANES), shaped(MATE_SENT, ROWS, LANES)],
        (surface, near, far),
    )
    mates = lax.all_gather(surface, "ply")
    sent = shaped(SENT_ALL, HALO, LANES)
    fresh, mate, extra, near, far = call(
        speed_kernel,
        [
            shaped(27, 2, ROWS, LANES),
            shaped(15, 2, ROWS, LANES),
            shaped(11, ROWS, LANES),
            sent,
            sent,
        ],
        (plate_state, damage, frame_mask, impact_mask, side, mates),
        scratch=[pltpu.VMEM((2, SENT, HALO, LANES), jnp.float32)] * 2,
    )
    far = lax.ppermute(far, "len", swap)
    near = lax.all_gather(near, "len", axis_index_groups=even)
    return call(
        last_kernel,
        shaped(1, 10, THICK, ROWS, LANES),
        (plate_state, extra, side, fresh, mate, near, far),
        scratch=[pltpu.VMEM((ALL, 2, ROWS + 2 * HALO, LANES), jnp.float32)],
    )


def solution(mesh):
    placed = (
        P("ply", None, None, "len", "hgt"),
        P("ply", None, "len", "hgt"),
        P("len", "hgt"),
        P("len", "hgt"),
    )
    return jax.shard_map(
        per_device,
        mesh=mesh,
        in_specs=placed,
        out_specs=P("ply", None, None, "len", "hgt"),
        check_vma=False,
    )
```

```python
import jax
import jax.numpy as jnp
from jax import lax
from jax.experimental import pallas as pl
from jax.experimental.pallas import tpu as pltpu
from jax.sharding import PartitionSpec as P

time_step = 0.25
softening = 0.15
damping = 1.0
stiffness = 2.0
pressure = 2.0

THICK = 8
ROWS = 16
LANES = 128
HALO = 8
STEP = time_step / 12.0

VX, VY, VZ, SXX, SYY, SZZ, SXY, SXZ, SYZ, SCALE = range(10)
DISP, KEEP, PUSH, OWN = 80, 81, 82, 83
SPARE = 83
MATE = 83
MATES = 10
ALL = MATE + MATES
M_VX, M_VY, M_VZ, M_W, M_XX, M_XY, M_XZ, M_FX, M_FY, M_FZ = range(MATE, ALL)

PICKS = [(VX, 0), (VY, 0), (VZ, 0), None, (SXX, 0), (SYY, 0), (SXY, 0), (SXZ, 0), (SYZ, 0)]
PICKS += [(f, depth) for depth in (1, 2) for f in (SXZ, SYZ, SZZ)]

PER_GROUP = 16
GROUPS = 6
MATE_SENT = MATES + 2

VMEM = pl.BlockSpec(memory_space=pltpu.VMEM)
MIB = 2**20


def at(field, z):
    return field * THICK + z


def fours():
    items = [(at(f, z), False) for f in (SXX, SXY, SXZ, SCALE) for z in range(THICK)]
    items += [(at(f, z), True) for f in (VX, VY, VZ) for z in range(THICK)]
    return items + [(p, False) for p in (M_XX, M_XY, M_XZ)]


def twos():
    items = [at(f, z) for f in (SYY, SZZ, SYZ, VX, VY, VZ) for z in range(THICK)]
    items += [M_VX, M_VY, M_VZ, M_W, M_FX, M_FY, M_FZ]
    return items + [DISP, KEEP, PUSH]


def travel(down):
    moves, row = [], 0
    for plane, new in fours():
        first = (10 if new else 12) if down else (2 if new else 0)
        moves.append((plane, first, 4, new, row // 8, row % 8))
        row += 4
    for plane in twos():
        moves.append((plane, 14 if down else 0, 2, False, row // 8, row % 8))
        row += 2
    return moves


SENT = -(-(4 * len(fours()) + 2 * len(twos())) // 8)
SENT_SIDES = -(-SENT // 8)
SENT_ALL = SENT + SENT_SIDES


def lanes_of(rows):
    return lax.broadcasted_iota(jnp.int32, (rows, LANES), 1)


def turn(x, by):
    by %= LANES
    return pltpu.roll(x, by, 1) if by else x


def pack_sides(planes):
    slot = lanes_of(planes[0].shape[0]) // 16
    packed = jnp.zeros(planes[0].shape, jnp.float32)
    for j, plane in enumerate(planes):
        packed = jnp.where(slot == j, turn(plane, HALO + 16 * j), packed)
    return packed


def unpack_side(packed, j):
    lane = lanes_of(packed.shape[0])
    side = turn(packed, -(HALO + 16 * j))
    return jnp.where((lane < HALO) | (lane >= LANES - HALO), side, 0.0)


def lane_shift(x, s):
    lane = lax.broadcasted_iota(jnp.int32, x.shape, 2)
    turned = pltpu.roll(x, (-s) % LANES, 2)
    other = jnp.concatenate([turned[1:2], turned[0:1]], axis=0)
    inside = lane < LANES - s if s > 0 else lane >= -s
    return jnp.where(inside, turned, other)


def along_height(x):
    near = lane_shift(x, 1) - lane_shift(x, -1)
    return 8.0 * near - (lane_shift(x, 2) - lane_shift(x, -2))


def along_length(look, plane, r0, n):
    near = look(plane, r0 + 1, n) - look(plane, r0 - 1, n)
    return 8.0 * near - (look(plane, r0 + 2, n) - look(plane, r0 - 2, n))


def through(look, field, z, r0, n):
    def layer(k):
        return look(at(field, k), r0, n) if 0 <= k < THICK else jnp.zeros((2, n, LANES), jnp.float32)

    return 8.0 * (layer(z + 1) - layer(z - 1)) - (layer(z + 2) - layer(z - 2))


def new_velocities(look, r0, n, front, put, with_mate):
    keep = look(KEEP, r0, n)

    def bonded(field):
        return jnp.where(front, look(at(field, THICK - 1), r0, n), look(at(field, 0), r0, n))

    mate = [look(p, r0, n) for p in (M_VX, M_VY, M_VZ, M_W)]
    pull = [
        damping * (mate[0] - bonded(VX)),
        damping * (mate[1] - bonded(VY)),
        stiffness * (mate[3] - look(DISP, r0, n)) + damping * (mate[2] - bonded(VZ)),
    ]
    pull = [time_step * p for p in pull]
    push = jnp.where(front, time_step * pressure, 0.0) * look(PUSH, r0, n)
    if with_mate:
        for f, (a, force) in enumerate(((M_XX, M_FX), (M_XY, M_FY), (M_XZ, M_FZ))):
            total = along_length(look, a, r0, n) + look(force, r0, n)
            put(M_VX + f, (mate[f] + STEP * total - pull[f]) * keep)
    for z in range(THICK):
        for f, (a, b, c) in enumerate(((SXX, SXY, SXZ), (SXY, SYY, SYZ), (SXZ, SYZ, SZZ))):
            total = (
                along_length(look, at(a, z), r0, n)
                + along_height(look(at(b, z), r0, n))
                + through(look, c, z, r0, n)
            )
            fresh = look(at(f, z), r0, n) + STEP * total
            if z == 0:
                fresh += jnp.where(front, 0.0, 1.0) * pull[f]
                if f == 2:
                    fresh += push
            if z == THICK - 1:
                fresh += jnp.where(front, 1.0, 0.0) * pull[f]
            put(at(f, z), fresh * keep)


def fetch_kernel(state, damage, frame, impact, near, far, again, tile, levels, held, struck, arrived):
    copies = [
        pltpu.make_async_copy(damage.at[0], levels, arrived.at[10]),
        pltpu.make_async_copy(frame, held, arrived.at[11]),
        pltpu.make_async_copy(impact, struck, arrived.at[12]),
    ]
    for f in range(10):
        first = SPARE if f == 9 else at(f, 0)
        copies.append(
            pltpu.make_async_copy(state.at[0, f], tile.at[pl.ds(first, THICK)], arrived.at[f])
        )
    for copy in copies:
        copy.start()
    for copy in (*copies[:3], copies[12]):
        copy.wait()
    front = lax.axis_index("ply") == 0
    even = lax.axis_index("hgt") % 2 == 0
    for z in range(THICK):
        tile[at(SCALE, z)] = 1.0 - softening * levels[z].astype(jnp.float32)
    tile[DISP] = jnp.where(front, tile[SPARE + THICK - 1], tile[SPARE])
    tile[KEEP] = (1 - held[...]).astype(jnp.float32)
    tile[PUSH] = struck[...].astype(jnp.float32)
    slot = lanes_of(ROWS) // HALO
    for g in range(GROUPS):
        for copy in copies[3 + 2 * g : min(5 + 2 * g, 12)]:
            copy.wait()
        first = jnp.zeros((ROWS, LANES), jnp.float32)
        last = first
        for j in range(min(PER_GROUP, OWN - g * PER_GROUP)):
            plane = tile[g * PER_GROUP + j]
            first = jnp.where(slot == j, turn(plane, HALO * j), first)
            last = jnp.where(slot == j, turn(plane, HALO * j + HALO), last)
        near[g] = again[g] = jnp.where(even, last, first)
        far[g] = jnp.where(even, first, last)


def side_kernel(state, high, far, low, side, surface):
    front = lax.axis_index("ply") == 0
    place = lax.axis_index("hgt")
    even = place % 2 == 0
    lane = lanes_of(ROWS)
    is_right = (lane < HALO) & (place < lax.axis_size("hgt") - 1)
    is_left = (lane >= LANES - HALO) & (place > 0)
    for g in range(GROUPS):
        near = jnp.where(place < lax.axis_size("hgt") // 2, low[g], high[g])
        from_right = jnp.where(even, near, far[g])
        from_left = jnp.where(even, far[g], near)
        for j in range(min(PER_GROUP, OWN - g * PER_GROUP)):
            r = turn(from_right, -HALO * j)
            m = turn(from_left, -HALO - HALO * j)
            side[g * PER_GROUP + j] = jnp.where(is_right, r, jnp.where(is_left, m, 0.0))
    full = []
    for k, pick in enumerate(PICKS):
        if pick is None:
            main = jnp.where(front, state[0, 9, THICK - 1], state[0, 9, 0])
            flank = side[DISP]
        else:
            f, less, more = pick[0], pick[1], THICK - 1 - pick[1]
            main = jnp.where(front, state[0, f, more], state[0, f, less])
            flank = jnp.where(front, side[at(f, more)], side[at(f, less)])
        full.append(jnp.stack([main, flank]))
    up = jnp.where(front, -1.0, 1.0)
    sent = full[:5] + full[6:8]
    for crossing, one, two in ((6, 9, 12), (5, 10, 13), (8, 11, 14)):
        sent.append(along_height(full[crossing]) + up * (8.0 * full[one] - full[two]))
    for k, planes in enumerate(sent):
        surface[k] = planes[0]
    flanks = [planes[1] for planes in sent]
    surface[MATES] = pack_sides(flanks[:8])
    surface[MATES + 1] = pack_sides(flanks[8:])


def speed_kernel(
    state, damage, frame, impact, side, mates, fresh, mate, extra, near, far, middle, flank
):
    front = lax.axis_index("ply") == 0
    for z in range(THICK):
        extra[z] = 1.0 - softening * damage[0, z].astype(jnp.float32)
    extra[DISP - 72] = jnp.where(front, state[0, 9, THICK - 1], state[0, 9, 0])
    extra[KEEP - 72] = (1 - frame[...]).astype(jnp.float32)
    extra[PUSH - 72] = impact[...].astype(jnp.float32)
    core = lax.axis_index("len") % 2
    other = jnp.where(front, 1, 0)
    for k in range(MATES):
        mate[k, 0] = mates[other, k]
        mate[k, 1] = unpack_side(mates[other, MATES + k // 8], k % 8)

    def look(plane, r, n):
        if plane >= MATE:
            return mate[plane - MATE, :, r : r + n, :]
        if plane >= 72:
            main = extra[plane - 72, r : r + n, :]
        else:
            main = state[0, plane // THICK, plane % THICK, r : r + n, :]
        return jnp.stack([main, side[plane, r : r + n, :]])

    def put(plane, value):
        fresh[plane if plane < 24 else 24 + plane - MATE, :, 2 : ROWS - 2, :] = value

    new_velocities(look, 2, ROWS - 4, front, put, True)

    for down in (0, 1):
        middle[down, SENT - 1] = jnp.zeros((HALO, LANES), jnp.float32)
        flank[down, SENT - 1] = jnp.zeros((HALO, LANES), jnp.float32)
        for plane, r, n, new, k, row in travel(down):
            value = fresh[plane, :, r : r + n, :] if new else look(plane, r, n)
            middle[down, k, row : row + n, :] = value[0]
            flank[down, k, row : row + n, :] = value[1]
    for out, way in ((near, 1 - core), (far, core)):
        for k in range(SENT):
            out[k] = middle[way, k]
        for g in range(SENT_SIDES):
            ks = range(8 * g, min(8 * g + 8, SENT))
            out[SENT + g] = pack_sides([flank[way, k] for k in ks])


def last_kernel(state, extra, side, fresh, mate, near, far, out, cells):
    front = lax.axis_index("ply") == 0
    index = lax.axis_index("len")
    upper = index % 2 == 0
    has_top = index > 0
    has_bottom = index < lax.axis_size("len") - 1

    for plane in range(OWN):
        if plane >= 72:
            main = extra[plane - 72]
        else:
            main = state[0, plane // THICK, plane % THICK]
        cells[plane, 0, HALO : HALO + ROWS, :] = main
        cells[plane, 1, HALO : HALO + ROWS, :] = side[plane]
    for k in range(MATES):
        cells[MATE + k, :, HALO : HALO + ROWS, :] = mate[k]
    for k in range(27):
        plane = k if k < 24 else MATE + k - 24
        cells[plane, :, HALO + 2 : HALO + ROWS - 2, :] = fresh[k, :, 2 : ROWS - 2, :]
    for down, there in ((1, has_top), (0, has_bottom)):

        def sent(k):
            first, second = (far[k], near[0, k]) if down else (near[1, k], far[k])
            return jnp.where(there, jnp.where(upper, first, second), 0.0)

        packed = [sent(SENT + g) for g in range(SENT_SIDES)]
        move = -ROWS if down else ROWS
        held = None
        for plane, r, n, _, k, row in travel(down):
            if k != held:
                held, main, flank = k, sent(k), unpack_side(packed[k // 8], k % 8)
            place = HALO + r + move
            cells[plane, 0, place : place + n, :] = main[row : row + n]
            cells[plane, 1, place : place + n, :] = flank[row : row + n]

    def look(plane, r, n):
        return cells[plane, :, HALO + r : HALO + r + n, :]

    def writer(r, n):
        def put(plane, value):
            cells[plane, :, HALO + r : HALO + r + n, :] = value

        return put

    for r in (-2, ROWS - 2):
        new_velocities(look, r, 4, front, writer(r, 4), True)
    r, n = -2, ROWS + 4
    put = writer(r, n)
    own_z = jnp.where(front, look(at(VZ, THICK - 1), r, n), look(at(VZ, 0), r, n))
    put(DISP, look(DISP, r, n) + time_step * own_z)
    put(M_W, look(M_W, r, n) + time_step * look(M_VZ, r, n))

    def changes(z, r, n, size):
        def length_of(f):
            return along_length(look, at(f, z), r, n)[:size]

        def height_of(f):
            return along_height(look(at(f, z), r, n))[:size]

        def depth_of(f):
            return through(look, f, z, r, n)[:size]

        factor = STEP * look(at(SCALE, z), r, n)[:size]
        xx, yy, zz = length_of(VX), height_of(VY), depth_of(VZ)
        whole = xx + yy + zz
        return (
            factor * (whole + 2.0 * xx),
            factor * (whole + 2.0 * yy),
            factor * (whole + 2.0 * zz),
            factor * (height_of(VX) + length_of(VY)),
            factor * (depth_of(VX) + length_of(VZ)),
            factor * (depth_of(VY) + height_of(VZ)),
        )

    r, n = -4, ROWS + 8
    put = writer(r, n)
    for z in range(THICK):
        for f, change in enumerate(changes(z, r, n, 2)):
            put(at(SXX + f, z), look(at(SXX + f, z), r, n) + change)
        out[0, 9, z] = state[0, 9, z] + time_step * look(at(VZ, z), 0, ROWS)[0]
    new_velocities(look, -2, ROWS + 4, front, writer(-2, ROWS + 4), False)
    for z in range(THICK):
        for f in range(3):
            out[0, f, z] = look(at(f, z), 0, ROWS)[0]
        for f, change in enumerate(changes(z, 0, ROWS, 1)):
            out[0, 3 + f, z] = look(at(SXX + f, z), 0, ROWS)[0] + change[0]
        out[0, 9, z] += time_step * look(at(VZ, z), 0, ROWS)[0]


def shaped(*shape):
    return jax.ShapeDtypeStruct(shape, jnp.float32)


def call(kernel, outs, args, limit=32 * MIB, space=pltpu.VMEM, scratch=()):
    return pl.pallas_call(
        kernel,
        out_shape=outs,
        in_specs=[pl.BlockSpec(memory_space=space)] * len(args),
        out_specs=jax.tree.map(lambda _: VMEM, outs),
        scratch_shapes=scratch,
        compiler_params=pltpu.CompilerParams(vmem_limit_bytes=limit),
    )(*args)


FETCH_LIMIT = 60 * MIB


def per_device(plate_state, damage, frame_mask, impact_mask):
    even = [[2 * i, 2 * i + 1] for i in range(8)]
    odd = [[2 * i + 1, (2 * i + 2) % 16] for i in range(8)]
    strips = shaped(GROUPS, ROWS, LANES)
    near, far, again = call(
        fetch_kernel,
        [strips, strips, strips],
        (plate_state, damage, frame_mask, impact_mask),
        limit=FETCH_LIMIT,
        space=pl.ANY,
        scratch=[
            pltpu.VMEM((OWN + THICK, ROWS, LANES), jnp.float32),
            pltpu.VMEM((THICK, ROWS, LANES), jnp.int32),
            pltpu.VMEM((ROWS, LANES), jnp.int32),
            pltpu.VMEM((ROWS, LANES), jnp.int32),
            pltpu.SemaphoreType.DMA((13,)),
        ],
    )
    swap = [(i, j) for pair in odd[:-1] for i, j in (pair, pair[::-1])]
    both = lambda pairs: [(i, j) for pair in pairs for i, j in (pair, pair[::-1])]
    high = lax.ppermute(near, "hgt", both(even[4:]))
    far = lax.ppermute(far, "hgt", swap)
    low = lax.ppermute(again, "hgt", both(even[:4]))
    side, surface = call(
        side_kernel,
        [shaped(OWN, ROWS, LANES), shaped(MATE_SENT, ROWS, LANES)],
        (plate_state, high, far, low),
    )
    mates = lax.all_gather(surface, "ply")
    sent = shaped(SENT_ALL, HALO, LANES)
    fresh, mate, extra, near, far = call(
        speed_kernel,
        [
            shaped(27, 2, ROWS, LANES),
            shaped(MATES, 2, ROWS, LANES),
            shaped(11, ROWS, LANES),
            sent,
            sent,
        ],
        (plate_state, damage, frame_mask, impact_mask, side, mates),
        scratch=[pltpu.VMEM((2, SENT, HALO, LANES), jnp.float32)] * 2,
    )
    far = lax.ppermute(far, "len", swap)
    near = lax.all_gather(near, "len", axis_index_groups=even)
    return call(
        last_kernel,
        shaped(1, 10, THICK, ROWS, LANES),
        (plate_state, extra, side, fresh, mate, near, far),
        scratch=[pltpu.VMEM((ALL, 2, ROWS + 2 * HALO, LANES), jnp.float32)],
    )


def solution(mesh):
    placed = (
        P("ply", None, None, "len", "hgt"),
        P("ply", None, "len", "hgt"),
        P("len", "hgt"),
        P("len", "hgt"),
    )
    return jax.shard_map(
        per_device,
        mesh=mesh,
        in_specs=placed,
        out_specs=P("ply", None, None, "len", "hgt"),
        check_vma=False,
    )
```

```python
import jax
import jax.numpy as jnp
from jax import lax
from jax.experimental import pallas as pl
from jax.experimental.pallas import tpu as pltpu
from jax.sharding import PartitionSpec as P

time_step = 0.25
softening = 0.15
damping = 1.0
stiffness = 2.0
pressure = 2.0

THICK = 8
ROWS = 16
LANES = 128
HALO = 8
STEP = time_step / 12.0

VX, VY, VZ, SXX, SYY, SZZ, SXY, SXZ, SYZ, SCALE = range(10)
SCALES, DISP, KEEP, PUSH, OWN = 72, 80, 81, 82, 83
LEAN = 72
MATE = 83
MATES = 10
ALL = MATE + MATES
M_VX, M_VY, M_VZ, M_W, M_XX, M_XY, M_XZ, M_FX, M_FY, M_FZ = range(MATE, ALL)

PICKS = [(VX, 0), (VY, 0), (VZ, 0), None, (SXX, 0), (SYY, 0), (SXY, 0), (SXZ, 0), (SYZ, 0)]
PICKS += [(f, depth) for depth in (1, 2) for f in (SXZ, SYZ, SZZ)]

PER_GROUP = 16
GROUPS = 6
MATE_SENT = MATES + 2

VMEM = pl.BlockSpec(memory_space=pltpu.VMEM)
MIB = 2**20


def at(field, z):
    return field * THICK + z


def fours():
    items = [(at(f, z), False) for f in (SXX, SXY, SXZ, SCALE) for z in range(THICK)]
    items += [(at(f, z), True) for f in (VX, VY, VZ) for z in range(THICK)]
    return items + [(p, False) for p in (M_XX, M_XY, M_XZ)]


def twos():
    items = [at(f, z) for f in (SYY, SZZ, SYZ, VX, VY, VZ) for z in range(THICK)]
    items += [M_VX, M_VY, M_VZ, M_W, M_FX, M_FY, M_FZ]
    return items + [DISP, KEEP, PUSH]


def travel(down):
    moves, row = [], 0
    for plane, new in fours():
        first = (10 if new else 12) if down else (2 if new else 0)
        moves.append((plane, first, 4, new, row // 8, row % 8))
        row += 4
    for plane in twos():
        moves.append((plane, 14 if down else 0, 2, False, row // 8, row % 8))
        row += 2
    return moves


SENT = -(-(4 * len(fours()) + 2 * len(twos())) // 8)
SENT_SIDES = -(-SENT // 8)
SENT_ALL = SENT + SENT_SIDES


def own_plane(tile, front, plane, rows=slice(0, ROWS)):
    if plane == DISP:
        return jnp.where(front, tile[LEAN + THICK - 1, rows, :], tile[LEAN, rows, :])
    if plane >= SCALES:
        plane += THICK - (plane > DISP)
    return tile[plane, rows, :]


def lanes_of(rows):
    return lax.broadcasted_iota(jnp.int32, (rows, LANES), 1)


def turn(x, by):
    by %= LANES
    return pltpu.roll(x, by, 1) if by else x


def pack_sides(planes):
    slot = lanes_of(planes[0].shape[0]) // 16
    packed = jnp.zeros(planes[0].shape, jnp.float32)
    for j, plane in enumerate(planes):
        packed = jnp.where(slot == j, turn(plane, HALO + 16 * j), packed)
    return packed


def unpack_side(packed, j):
    lane = lanes_of(packed.shape[0])
    side = turn(packed, -(HALO + 16 * j))
    return jnp.where((lane < HALO) | (lane >= LANES - HALO), side, 0.0)


def lane_shift(x, s):
    lane = lax.broadcasted_iota(jnp.int32, x.shape, 2)
    turned = pltpu.roll(x, (-s) % LANES, 2)
    other = jnp.concatenate([turned[1:2], turned[0:1]], axis=0)
    inside = lane < LANES - s if s > 0 else lane >= -s
    return jnp.where(inside, turned, other)


def along_height(x):
    near = lane_shift(x, 1) - lane_shift(x, -1)
    return 8.0 * near - (lane_shift(x, 2) - lane_shift(x, -2))


def along_length(look, plane, r0, n):
    near = look(plane, r0 + 1, n) - look(plane, r0 - 1, n)
    return 8.0 * near - (look(plane, r0 + 2, n) - look(plane, r0 - 2, n))


def through(look, field, z, r0, n):
    def layer(k):
        return look(at(field, k), r0, n) if 0 <= k < THICK else jnp.zeros((2, n, LANES), jnp.float32)

    return 8.0 * (layer(z + 1) - layer(z - 1)) - (layer(z + 2) - layer(z - 2))


def new_velocities(look, r0, n, front, put, with_mate):
    keep = look(KEEP, r0, n)

    def bonded(field):
        return jnp.where(front, look(at(field, THICK - 1), r0, n), look(at(field, 0), r0, n))

    mate = [look(p, r0, n) for p in (M_VX, M_VY, M_VZ, M_W)]
    pull = [
        damping * (mate[0] - bonded(VX)),
        damping * (mate[1] - bonded(VY)),
        stiffness * (mate[3] - look(DISP, r0, n)) + damping * (mate[2] - bonded(VZ)),
    ]
    pull = [time_step * p for p in pull]
    push = jnp.where(front, time_step * pressure, 0.0) * look(PUSH, r0, n)
    if with_mate:
        for f, (a, force) in enumerate(((M_XX, M_FX), (M_XY, M_FY), (M_XZ, M_FZ))):
            total = along_length(look, a, r0, n) + look(force, r0, n)
            put(M_VX + f, (mate[f] + STEP * total - pull[f]) * keep)
    for z in range(THICK):
        for f, (a, b, c) in enumerate(((SXX, SXY, SXZ), (SXY, SYY, SYZ), (SXZ, SYZ, SZZ))):
            total = (
                along_length(look, at(a, z), r0, n)
                + along_height(look(at(b, z), r0, n))
                + through(look, c, z, r0, n)
            )
            fresh = look(at(f, z), r0, n) + STEP * total
            if z == 0:
                fresh += jnp.where(front, 0.0, 1.0) * pull[f]
                if f == 2:
                    fresh += push
            if z == THICK - 1:
                fresh += jnp.where(front, 1.0, 0.0) * pull[f]
            put(at(f, z), fresh * keep)


def strip_kernel(tile, near, far, again):
    front = lax.axis_index("ply") == 0
    even = lax.axis_index("hgt") % 2 == 0
    slot = lanes_of(ROWS) // HALO
    for g in range(GROUPS):
        first = jnp.zeros((ROWS, LANES), jnp.float32)
        last = first
        for j in range(min(PER_GROUP, OWN - g * PER_GROUP)):
            plane = own_plane(tile, front, g * PER_GROUP + j)
            plane = turn(plane, HALO * j + HALO)
            first = jnp.where(slot == (j + 1) % PER_GROUP, plane, first)
            last = jnp.where(slot == j, plane, last)
        first = turn(first, -HALO)
        near[g] = again[g] = jnp.where(even, last, first)
        far[g] = jnp.where(even, first, last)


def side_kernel(tile, high, far, low, side, surface):
    front = lax.axis_index("ply") == 0
    place = lax.axis_index("hgt")
    even = place % 2 == 0
    lane = lanes_of(ROWS)
    is_right = (lane < HALO) & (place < lax.axis_size("hgt") - 1)
    is_left = (lane >= LANES - HALO) & (place > 0)
    for g in range(GROUPS):
        near = jnp.where(place < lax.axis_size("hgt") // 2, low[g], high[g])
        from_right = jnp.where(even, near, far[g])
        from_left = jnp.where(even, far[g], near)
        for j in range(min(PER_GROUP, OWN - g * PER_GROUP)):
            r = turn(from_right, -HALO * j)
            m = turn(from_left, -HALO - HALO * j)
            side[g * PER_GROUP + j] = jnp.where(is_right, r, jnp.where(is_left, m, 0.0))
    full = []
    for k, pick in enumerate(PICKS):
        if pick is None:
            main = own_plane(tile, front, DISP)
            flank = side[DISP]
        else:
            f, less, more = pick[0], pick[1], THICK - 1 - pick[1]
            main = jnp.where(front, tile[at(f, more)], tile[at(f, less)])
            flank = jnp.where(front, side[at(f, more)], side[at(f, less)])
        full.append(jnp.stack([main, flank]))
    up = jnp.where(front, -1.0, 1.0)
    sent = full[:5] + full[6:8]
    for crossing, one, two in ((6, 9, 12), (5, 10, 13), (8, 11, 14)):
        sent.append(along_height(full[crossing]) + up * (8.0 * full[one] - full[two]))
    for k, planes in enumerate(sent):
        surface[k] = planes[0]
    flanks = [planes[1] for planes in sent]
    surface[MATES] = pack_sides(flanks[:8])
    surface[MATES + 1] = pack_sides(flanks[8:])


def speed_kernel(
    tile, side, mates, fresh, mate, near, far, middle, flank
):
    front = lax.axis_index("ply") == 0
    core = lax.axis_index("len") % 2
    other = jnp.where(front, 1, 0)
    for k in range(MATES):
        mate[k, 0] = mates[other, k]
        mate[k, 1] = unpack_side(mates[other, MATES + k // 8], k % 8)

    def look(plane, r, n):
        if plane >= MATE:
            return mate[plane - MATE, :, r : r + n, :]
        main = own_plane(tile, front, plane, slice(r, r + n))
        return jnp.stack([main, side[plane, r : r + n, :]])

    def put(plane, value):
        fresh[plane if plane < 24 else 24 + plane - MATE, :, 2 : ROWS - 2, :] = value

    new_velocities(look, 2, ROWS - 4, front, put, True)

    for down in (0, 1):
        middle[down, SENT - 1] = jnp.zeros((HALO, LANES), jnp.float32)
        flank[down, SENT - 1] = jnp.zeros((HALO, LANES), jnp.float32)
        for plane, r, n, new, k, row in travel(down):
            value = fresh[plane, :, r : r + n, :] if new else look(plane, r, n)
            middle[down, k, row : row + n, :] = value[0]
            flank[down, k, row : row + n, :] = value[1]
    for out, way in ((near, 1 - core), (far, core)):
        for k in range(SENT):
            out[k] = middle[way, k]
        for g in range(SENT_SIDES):
            ks = range(8 * g, min(8 * g + 8, SENT))
            out[SENT + g] = pack_sides([flank[way, k] for k in ks])


def last_kernel(tile, side, fresh, mate, near, far, out, cells):
    front = lax.axis_index("ply") == 0
    index = lax.axis_index("len")
    upper = index % 2 == 0
    has_top = index > 0
    has_bottom = index < lax.axis_size("len") - 1

    for plane in range(OWN):
        cells[plane, 0, HALO : HALO + ROWS, :] = own_plane(tile, front, plane)
        cells[plane, 1, HALO : HALO + ROWS, :] = side[plane]
    for k in range(MATES):
        cells[MATE + k, :, HALO : HALO + ROWS, :] = mate[k]
    for k in range(27):
        plane = k if k < 24 else MATE + k - 24
        cells[plane, :, HALO + 2 : HALO + ROWS - 2, :] = fresh[k, :, 2 : ROWS - 2, :]
    for down, there in ((1, has_top), (0, has_bottom)):

        def sent(k):
            first, second = (far[k], near[0, k]) if down else (near[1, k], far[k])
            return jnp.where(there, jnp.where(upper, first, second), 0.0)

        packed = [sent(SENT + g) for g in range(SENT_SIDES)]
        move = -ROWS if down else ROWS
        held = None
        for plane, r, n, _, k, row in travel(down):
            if k != held:
                held, main, flank = k, sent(k), unpack_side(packed[k // 8], k % 8)
            place = HALO + r + move
            cells[plane, 0, place : place + n, :] = main[row : row + n]
            cells[plane, 1, place : place + n, :] = flank[row : row + n]

    def look(plane, r, n):
        return cells[plane, :, HALO + r : HALO + r + n, :]

    def writer(r, n):
        def put(plane, value):
            cells[plane, :, HALO + r : HALO + r + n, :] = value

        return put

    for r in (-2, ROWS - 2):
        new_velocities(look, r, 4, front, writer(r, 4), True)
    r, n = -2, ROWS + 4
    put = writer(r, n)
    own_z = jnp.where(front, look(at(VZ, THICK - 1), r, n), look(at(VZ, 0), r, n))
    put(DISP, look(DISP, r, n) + time_step * own_z)
    put(M_W, look(M_W, r, n) + time_step * look(M_VZ, r, n))

    def changes(z, r, n, size):
        def length_of(f):
            return along_length(look, at(f, z), r, n)[:size]

        def height_of(f):
            return along_height(look(at(f, z), r, n))[:size]

        def depth_of(f):
            return through(look, f, z, r, n)[:size]

        factor = STEP * look(at(SCALE, z), r, n)[:size]
        xx, yy, zz = length_of(VX), height_of(VY), depth_of(VZ)
        whole = xx + yy + zz
        return (
            factor * (whole + 2.0 * xx),
            factor * (whole + 2.0 * yy),
            factor * (whole + 2.0 * zz),
            factor * (height_of(VX) + length_of(VY)),
            factor * (depth_of(VX) + length_of(VZ)),
            factor * (depth_of(VY) + height_of(VZ)),
        )

    r, n = -4, ROWS + 8
    put = writer(r, n)
    for z in range(THICK):
        for f, change in enumerate(changes(z, r, n, 2)):
            put(at(SXX + f, z), look(at(SXX + f, z), r, n) + change)
        out[0, 9, z] = tile[LEAN + z] + time_step * look(at(VZ, z), 0, ROWS)[0]
    new_velocities(look, -2, ROWS + 4, front, writer(-2, ROWS + 4), False)
    for z in range(THICK):
        for f in range(3):
            out[0, f, z] = look(at(f, z), 0, ROWS)[0]
        for f, change in enumerate(changes(z, 0, ROWS, 1)):
            out[0, 3 + f, z] = look(at(SXX + f, z), 0, ROWS)[0] + change[0]
        out[0, 9, z] += time_step * look(at(VZ, z), 0, ROWS)[0]


def shaped(*shape):
    return jax.ShapeDtypeStruct(shape, jnp.float32)


def call(kernel, outs, args, limit=32 * MIB, space=pltpu.VMEM, scratch=()):
    return pl.pallas_call(
        kernel,
        out_shape=outs,
        in_specs=[pl.BlockSpec(memory_space=space)] * len(args),
        out_specs=jax.tree.map(lambda _: VMEM, outs),
        scratch_shapes=scratch,
        compiler_params=pltpu.CompilerParams(vmem_limit_bytes=limit),
    )(*args)


def per_device(plate_state, damage, frame_mask, impact_mask):
    even = [[2 * i, 2 * i + 1] for i in range(8)]
    odd = [[2 * i + 1, (2 * i + 2) % 16] for i in range(8)]
    strips = shaped(GROUPS, ROWS, LANES)
    tile = jnp.zeros((90, ROWS, LANES), jnp.float32)
    tile = lax.dynamic_update_slice(tile, plate_state.reshape(80, ROWS, LANES), (0, 0, 0))
    tile, damage, frame_mask, impact_mask = lax.optimization_barrier(
        (tile, damage, frame_mask, impact_mask)
    )
    whole = jnp.concatenate([damage[0], frame_mask[None], impact_mask[None]])
    which = lax.broadcasted_iota(jnp.int32, whole.shape, 0)
    slope = jnp.where(which < THICK, -softening, jnp.where(which == THICK, -1.0, 1.0))
    extra = jnp.where(which > THICK, 0.0, 1.0) + slope * whole.astype(jnp.float32)
    tile = lax.dynamic_update_slice(tile, extra, (80, 0, 0))
    near, far, again = call(strip_kernel, [strips, strips, strips], (tile,))
    swap = [(i, j) for pair in odd[:-1] for i, j in (pair, pair[::-1])]
    both = lambda pairs: [(i, j) for pair in pairs for i, j in (pair, pair[::-1])]
    high = lax.ppermute(near, "hgt", both(even[4:]))
    far = lax.ppermute(far, "hgt", swap)
    low = lax.ppermute(again, "hgt", both(even[:4]))
    side, surface = call(
        side_kernel,
        [shaped(OWN, ROWS, LANES), shaped(MATE_SENT, ROWS, LANES)],
        (tile, high, far, low),
    )
    mates = lax.all_gather(surface, "ply")
    sent = shaped(SENT_ALL, HALO, LANES)
    fresh, mate, near, far = call(
        speed_kernel,
        [
            shaped(27, 2, ROWS, LANES),
            shaped(MATES, 2, ROWS, LANES),
            sent,
            sent,
        ],
        (tile, side, mates),
        scratch=[pltpu.VMEM((2, SENT, HALO, LANES), jnp.float32)] * 2,
    )
    far = lax.ppermute(far, "len", swap)
    near = lax.all_gather(near, "len", axis_index_groups=even)
    return call(
        last_kernel,
        shaped(1, 10, THICK, ROWS, LANES),
        (tile, side, fresh, mate, near, far),
        scratch=[pltpu.VMEM((ALL, 2, ROWS + 2 * HALO, LANES), jnp.float32)],
    )


def solution(mesh):
    placed = (
        P("ply", None, None, "len", "hgt"),
        P("ply", None, "len", "hgt"),
        P("len", "hgt"),
        P("len", "hgt"),
    )
    return jax.shard_map(
        per_device,
        mesh=mesh,
        in_specs=placed,
        out_specs=P("ply", None, None, "len", "hgt"),
        check_vma=False,
    )
```

```python
import jax
import jax.numpy as jnp
from jax import lax
from jax.experimental import pallas as pl
from jax.experimental.pallas import tpu as pltpu
from jax.sharding import PartitionSpec as P

time_step = 0.25
softening = 0.15
damping = 1.0
stiffness = 2.0
pressure = 2.0

THICK = 8
ROWS = 16
LANES = 128
HALO = 8
STEP = time_step / 12.0

VX, VY, VZ, SXX, SYY, SZZ, SXY, SXZ, SYZ, SCALE = range(10)
SCALES, DISP, KEEP, PUSH, OWN = 72, 80, 81, 82, 83
LEAN = 72
MATE = 83
MATES = 10
ALL = MATE + MATES
M_VX, M_VY, M_VZ, M_W, M_XX, M_XY, M_XZ, M_FX, M_FY, M_FZ = range(MATE, ALL)

PICKS = [(VX, 0), (VY, 0), (VZ, 0), None, (SXX, 0), (SYY, 0), (SXY, 0), (SXZ, 0), (SYZ, 0)]
PICKS += [(f, depth) for depth in (1, 2) for f in (SXZ, SYZ, SZZ)]

PER_GROUP = 16
GROUPS = 6
MATE_SENT = MATES + 2

VMEM = pl.BlockSpec(memory_space=pltpu.VMEM)
MIB = 2**20


def at(field, z):
    return field * THICK + z


def fours():
    items = [(at(f, z), False) for f in (SXX, SXY, SXZ, SCALE) for z in range(THICK)]
    items += [(at(f, z), True) for f in (VX, VY, VZ) for z in range(THICK)]
    return items + [(p, False) for p in (M_XX, M_XY, M_XZ)]


def twos():
    items = [at(f, z) for f in (SYY, SZZ, SYZ, VX, VY, VZ) for z in range(THICK)]
    items += [M_VX, M_VY, M_VZ, M_W, M_FX, M_FY, M_FZ]
    return items + [DISP, KEEP, PUSH]


def travel(down):
    moves, row = [], 0
    for plane, new in fours():
        first = (10 if new else 12) if down else (2 if new else 0)
        moves.append((plane, first, 4, new, row // 8, row % 8))
        row += 4
    for plane in twos():
        moves.append((plane, 14 if down else 0, 2, False, row // 8, row % 8))
        row += 2
    return moves


SENT = -(-(4 * len(fours()) + 2 * len(twos())) // 8)
SENT_SIDES = -(-SENT // 8)
SENT_ALL = SENT + SENT_SIDES


def own_plane(tile, front, plane, rows=slice(0, ROWS)):
    if plane == DISP:
        return jnp.where(front, tile[LEAN + THICK - 1, rows, :], tile[LEAN, rows, :])
    if plane < SCALES:
        return tile[plane, rows, :]
    given = tile[plane + THICK - (plane > DISP), rows, :]
    if plane < DISP:
        return 1.0 - softening * given
    return 1.0 - given if plane == KEEP else given


def lanes_of(rows):
    return lax.broadcasted_iota(jnp.int32, (rows, LANES), 1)


def turn(x, by):
    by %= LANES
    return pltpu.roll(x, by, 1) if by else x


def pack_sides(planes):
    slot = lanes_of(planes[0].shape[0]) // 16
    packed = jnp.zeros(planes[0].shape, jnp.float32)
    for j, plane in enumerate(planes):
        packed = jnp.where(slot == j, turn(plane, HALO + 16 * j), packed)
    return packed


def unpack_side(packed, j):
    lane = lanes_of(packed.shape[0])
    side = turn(packed, -(HALO + 16 * j))
    return jnp.where((lane < HALO) | (lane >= LANES - HALO), side, 0.0)


def lane_shift(x, s):
    lane = lax.broadcasted_iota(jnp.int32, x.shape, 2)
    turned = pltpu.roll(x, (-s) % LANES, 2)
    other = jnp.concatenate([turned[1:2], turned[0:1]], axis=0)
    inside = lane < LANES - s if s > 0 else lane >= -s
    return jnp.where(inside, turned, other)


def along_height(x):
    near = lane_shift(x, 1) - lane_shift(x, -1)
    return 8.0 * near - (lane_shift(x, 2) - lane_shift(x, -2))


def along_length(look, plane, r0, n):
    near = look(plane, r0 + 1, n) - look(plane, r0 - 1, n)
    return 8.0 * near - (look(plane, r0 + 2, n) - look(plane, r0 - 2, n))


def through(look, field, z, r0, n):
    def layer(k):
        return look(at(field, k), r0, n) if 0 <= k < THICK else jnp.zeros((2, n, LANES), jnp.float32)

    return 8.0 * (layer(z + 1) - layer(z - 1)) - (layer(z + 2) - layer(z - 2))


def new_velocities(look, r0, n, front, put, with_mate):
    keep = look(KEEP, r0, n)

    def bonded(field):
        return jnp.where(front, look(at(field, THICK - 1), r0, n), look(at(field, 0), r0, n))

    mate = [look(p, r0, n) for p in (M_VX, M_VY, M_VZ, M_W)]
    pull = [
        damping * (mate[0] - bonded(VX)),
        damping * (mate[1] - bonded(VY)),
        stiffness * (mate[3] - look(DISP, r0, n)) + damping * (mate[2] - bonded(VZ)),
    ]
    pull = [time_step * p for p in pull]
    push = jnp.where(front, time_step * pressure, 0.0) * look(PUSH, r0, n)
    if with_mate:
        for f, (a, force) in enumerate(((M_XX, M_FX), (M_XY, M_FY), (M_XZ, M_FZ))):
            total = along_length(look, a, r0, n) + look(force, r0, n)
            put(M_VX + f, (mate[f] + STEP * total - pull[f]) * keep)
    for z in range(THICK):
        for f, (a, b, c) in enumerate(((SXX, SXY, SXZ), (SXY, SYY, SYZ), (SXZ, SYZ, SZZ))):
            total = (
                along_length(look, at(a, z), r0, n)
                + along_height(look(at(b, z), r0, n))
                + through(look, c, z, r0, n)
            )
            fresh = look(at(f, z), r0, n) + STEP * total
            if z == 0:
                fresh += jnp.where(front, 0.0, 1.0) * pull[f]
                if f == 2:
                    fresh += push
            if z == THICK - 1:
                fresh += jnp.where(front, 1.0, 0.0) * pull[f]
            put(at(f, z), fresh * keep)


def strip_kernel(tile, near, far, again):
    front = lax.axis_index("ply") == 0
    even = lax.axis_index("hgt") % 2 == 0
    slot = lanes_of(ROWS) // HALO
    for g in range(GROUPS):
        first = jnp.zeros((ROWS, LANES), jnp.float32)
        last = first
        for j in range(min(PER_GROUP, OWN - g * PER_GROUP)):
            plane = own_plane(tile, front, g * PER_GROUP + j)
            plane = turn(plane, HALO * j + HALO)
            first = jnp.where(slot == (j + 1) % PER_GROUP, plane, first)
            last = jnp.where(slot == j, plane, last)
        first = turn(first, -HALO)
        near[g] = again[g] = jnp.where(even, last, first)
        far[g] = jnp.where(even, first, last)


def side_kernel(tile, high, far, low, side, surface):
    front = lax.axis_index("ply") == 0
    place = lax.axis_index("hgt")
    even = place % 2 == 0
    lane = lanes_of(ROWS)
    is_right = (lane < HALO) & (place < lax.axis_size("hgt") - 1)
    is_left = (lane >= LANES - HALO) & (place > 0)
    for g in range(GROUPS):
        near = jnp.where(place < lax.axis_size("hgt") // 2, low[g], high[g])
        from_right = jnp.where(even, near, far[g])
        from_left = jnp.where(even, far[g], near)
        for j in range(min(PER_GROUP, OWN - g * PER_GROUP)):
            r = turn(from_right, -HALO * j)
            m = turn(from_left, -HALO - HALO * j)
            side[g * PER_GROUP + j] = jnp.where(is_right, r, jnp.where(is_left, m, 0.0))
    full = []
    for k, pick in enumerate(PICKS):
        if pick is None:
            main = own_plane(tile, front, DISP)
            flank = side[DISP]
        else:
            f, less, more = pick[0], pick[1], THICK - 1 - pick[1]
            main = jnp.where(front, tile[at(f, more)], tile[at(f, less)])
            flank = jnp.where(front, side[at(f, more)], side[at(f, less)])
        full.append(jnp.stack([main, flank]))
    up = jnp.where(front, -1.0, 1.0)
    sent = full[:5] + full[6:8]
    for crossing, one, two in ((6, 9, 12), (5, 10, 13), (8, 11, 14)):
        sent.append(along_height(full[crossing]) + up * (8.0 * full[one] - full[two]))
    for k, planes in enumerate(sent):
        surface[k] = planes[0]
    flanks = [planes[1] for planes in sent]
    surface[MATES] = pack_sides(flanks[:8])
    surface[MATES + 1] = pack_sides(flanks[8:])


def speed_kernel(
    tile, side, mates, fresh, mate, near, far, middle, flank
):
    front = lax.axis_index("ply") == 0
    core = lax.axis_index("len") % 2
    other = jnp.where(front, 1, 0)
    for k in range(MATES):
        mate[k, 0] = mates[other, k]
        mate[k, 1] = unpack_side(mates[other, MATES + k // 8], k % 8)

    def look(plane, r, n):
        if plane >= MATE:
            return mate[plane - MATE, :, r : r + n, :]
        main = own_plane(tile, front, plane, slice(r, r + n))
        return jnp.stack([main, side[plane, r : r + n, :]])

    def put(plane, value):
        fresh[plane if plane < 24 else 24 + plane - MATE, :, 2 : ROWS - 2, :] = value

    new_velocities(look, 2, ROWS - 4, front, put, True)

    for down in (0, 1):
        middle[down, SENT - 1] = jnp.zeros((HALO, LANES), jnp.float32)
        flank[down, SENT - 1] = jnp.zeros((HALO, LANES), jnp.float32)
        for plane, r, n, new, k, row in travel(down):
            value = fresh[plane, :, r : r + n, :] if new else look(plane, r, n)
            middle[down, k, row : row + n, :] = value[0]
            flank[down, k, row : row + n, :] = value[1]
    for out, way in ((near, 1 - core), (far, core)):
        for k in range(SENT):
            out[k] = middle[way, k]
        for g in range(SENT_SIDES):
            ks = range(8 * g, min(8 * g + 8, SENT))
            out[SENT + g] = pack_sides([flank[way, k] for k in ks])


def last_kernel(tile, side, fresh, mate, near, far, out, cells):
    front = lax.axis_index("ply") == 0
    index = lax.axis_index("len")
    upper = index % 2 == 0
    has_top = index > 0
    has_bottom = index < lax.axis_size("len") - 1

    for plane in range(OWN):
        cells[plane, 0, HALO : HALO + ROWS, :] = own_plane(tile, front, plane)
        cells[plane, 1, HALO : HALO + ROWS, :] = side[plane]
    for k in range(MATES):
        cells[MATE + k, :, HALO : HALO + ROWS, :] = mate[k]
    for k in range(27):
        plane = k if k < 24 else MATE + k - 24
        cells[plane, :, HALO + 2 : HALO + ROWS - 2, :] = fresh[k, :, 2 : ROWS - 2, :]
    for down, there in ((1, has_top), (0, has_bottom)):

        def sent(k):
            first, second = (far[k], near[0, k]) if down else (near[1, k], far[k])
            return jnp.where(there, jnp.where(upper, first, second), 0.0)

        packed = [sent(SENT + g) for g in range(SENT_SIDES)]
        move = -ROWS if down else ROWS
        held = None
        for plane, r, n, _, k, row in travel(down):
            if k != held:
                held, main, flank = k, sent(k), unpack_side(packed[k // 8], k % 8)
            place = HALO + r + move
            cells[plane, 0, place : place + n, :] = main[row : row + n]
            cells[plane, 1, place : place + n, :] = flank[row : row + n]

    def look(plane, r, n):
        return cells[plane, :, HALO + r : HALO + r + n, :]

    def writer(r, n):
        def put(plane, value):
            cells[plane, :, HALO + r : HALO + r + n, :] = value

        return put

    for r in (-2, ROWS - 2):
        new_velocities(look, r, 4, front, writer(r, 4), True)
    r, n = -2, ROWS + 4
    put = writer(r, n)
    own_z = jnp.where(front, look(at(VZ, THICK - 1), r, n), look(at(VZ, 0), r, n))
    put(DISP, look(DISP, r, n) + time_step * own_z)
    put(M_W, look(M_W, r, n) + time_step * look(M_VZ, r, n))

    def changes(z, r, n, size):
        def length_of(f):
            return along_length(look, at(f, z), r, n)[:size]

        def height_of(f):
            return along_height(look(at(f, z), r, n))[:size]

        def depth_of(f):
            return through(look, f, z, r, n)[:size]

        factor = STEP * look(at(SCALE, z), r, n)[:size]
        xx, yy, zz = length_of(VX), height_of(VY), depth_of(VZ)
        whole = xx + yy + zz
        return (
            factor * (whole + 2.0 * xx),
            factor * (whole + 2.0 * yy),
            factor * (whole + 2.0 * zz),
            factor * (height_of(VX) + length_of(VY)),
            factor * (depth_of(VX) + length_of(VZ)),
            factor * (depth_of(VY) + height_of(VZ)),
        )

    r, n = -4, ROWS + 8
    put = writer(r, n)
    for z in range(THICK):
        for f, change in enumerate(changes(z, r, n, 2)):
            put(at(SXX + f, z), look(at(SXX + f, z), r, n) + change)
        out[0, 9, z] = tile[LEAN + z] + time_step * look(at(VZ, z), 0, ROWS)[0]
    new_velocities(look, -2, ROWS + 4, front, writer(-2, ROWS + 4), False)
    for z in range(THICK):
        for f in range(3):
            out[0, f, z] = look(at(f, z), 0, ROWS)[0]
        for f, change in enumerate(changes(z, 0, ROWS, 1)):
            out[0, 3 + f, z] = look(at(SXX + f, z), 0, ROWS)[0] + change[0]
        out[0, 9, z] += time_step * look(at(VZ, z), 0, ROWS)[0]


def shaped(*shape):
    return jax.ShapeDtypeStruct(shape, jnp.float32)


def call(kernel, outs, args, limit=32 * MIB, space=pltpu.VMEM, scratch=()):
    return pl.pallas_call(
        kernel,
        out_shape=outs,
        in_specs=[pl.BlockSpec(memory_space=space)] * len(args),
        out_specs=jax.tree.map(lambda _: VMEM, outs),
        scratch_shapes=scratch,
        compiler_params=pltpu.CompilerParams(vmem_limit_bytes=limit),
    )(*args)


def per_device(plate_state, damage, frame_mask, impact_mask):
    even = [[2 * i, 2 * i + 1] for i in range(8)]
    odd = [[2 * i + 1, (2 * i + 2) % 16] for i in range(8)]
    strips = shaped(GROUPS, ROWS, LANES)
    tile = jnp.zeros((90, ROWS, LANES), jnp.float32)
    tile = lax.dynamic_update_slice(tile, plate_state.reshape(80, ROWS, LANES), (0, 0, 0))
    tile, damage, frame_mask, impact_mask = lax.optimization_barrier(
        (tile, damage, frame_mask, impact_mask)
    )
    whole = jnp.concatenate([damage[0], frame_mask[None], impact_mask[None]])
    extra = whole.astype(jnp.float32)
    tile = lax.dynamic_update_slice(tile, extra, (80, 0, 0))
    near, far, again = call(strip_kernel, [strips, strips, strips], (tile,))
    swap = [(i, j) for pair in odd[:-1] for i, j in (pair, pair[::-1])]
    both = lambda pairs: [(i, j) for pair in pairs for i, j in (pair, pair[::-1])]
    high = lax.ppermute(near, "hgt", both(even[4:]))
    far = lax.ppermute(far, "hgt", swap)
    low = lax.ppermute(again, "hgt", both(even[:4]))
    side, surface = call(
        side_kernel,
        [shaped(OWN, ROWS, LANES), shaped(MATE_SENT, ROWS, LANES)],
        (tile, high, far, low),
    )
    mates = lax.all_gather(surface, "ply")
    sent = shaped(SENT_ALL, HALO, LANES)
    fresh, mate, near, far = call(
        speed_kernel,
        [
            shaped(27, 2, ROWS, LANES),
            shaped(MATES, 2, ROWS, LANES),
            sent,
            sent,
        ],
        (tile, side, mates),
        scratch=[pltpu.VMEM((2, SENT, HALO, LANES), jnp.float32)] * 2,
    )
    far = lax.ppermute(far, "len", swap)
    near = lax.all_gather(near, "len", axis_index_groups=even)
    return call(
        last_kernel,
        shaped(1, 10, THICK, ROWS, LANES),
        (tile, side, fresh, mate, near, far),
        scratch=[pltpu.VMEM((ALL, 2, ROWS + 2 * HALO, LANES), jnp.float32)],
    )


def solution(mesh):
    placed = (
        P("ply", None, None, "len", "hgt"),
        P("ply", None, "len", "hgt"),
        P("len", "hgt"),
        P("len", "hgt"),
    )
    return jax.shard_map(
        per_device,
        mesh=mesh,
        in_specs=placed,
        out_specs=P("ply", None, None, "len", "hgt"),
        check_vma=False,
    )
```
